32 devices in a mesh: seq: 8 (over z, y), dp: 4 (over x, core).
Axes of the slice: x: 2, y: 2, z: 4, core: 2. Of those that a mesh axis runs over, the one named last changes fastest.
Arguments:
- inputs: float32 [4, 4096, 256], P('dp', 'seq'), may hold values from -6 to 6
- out_cotangent: float32 [4, 4096, 256], P('dp', 'seq'), may hold values from -6 to 6
- skip_cotangent: float32 [4, 4096, 256], P('dp', 'seq'), may hold values from -6 to 6
- convolution_weight: float32 [2, 512, 1024], replicated, may hold values from -0.25 to 0.25
- convolution_bias: float32 [2, 1024], replicated, may hold values from -3 to 3
- output_weight: float32 [2, 512, 512], replicated, may hold values from -0.25 to 0.25
Outputs:
- input_grad: float32 [4, 4096, 256], P('dp', 'seq')
- conv_grad: float32 [1024, 1024], P(('seq', 'dp'))
- out_grad: float32 [1024, 512], P(('seq', 'dp'))
- bias_grad: float32 [2048], P(('seq', 'dp'))
The draws below stay inside these ranges and needn't reach their ends.
All inputs are finite; a program needn't handle non-finite values.
Results may differ from the reference program's by a relative error of at most 0.00025.
Values sent between devices are 32-bit elements; how exact they have to be, the bound alone decides.
A program may use at most 128 MiB of HBM per device.

```python
import math
import jax
import jax.numpy as jnp
from jax import lax

R = 256
G = 512
LAYERS = 2
FIRST_DILATION = 256
SECOND_DILATION = 512
LENGTH = 4096
SEQS = 4


def shard_levels(stream_key, shape, pieces, least, high):
    level, own = 1.0, jax.random.fold_in(stream_key, 6)
    for dim, shards_of in pieces:
        heights = jnp.exp(jax.random.uniform(jax.random.fold_in(own, dim), (shards_of,), jnp.float32, least / len(pieces), high / len(pieces)))
        level = level * jnp.repeat(heights, shape[dim] // shards_of).reshape([-1 if axis == dim else 1 for axis in range(len(shape))])
    return level


def scatter_about(stream_key, extent, width, limit, split=(), dtype=jnp.bfloat16):
    factor_of = shard_levels(stream_key, extent, split, -0.22, 0.18) if split else 1.0
    values = jax.random.normal(stream_key, extent, jnp.float32) * width * factor_of
    return jnp.minimum(jnp.maximum(values, -limit), limit).astype(dtype)


def setup_inputs(seed: int = 0) -> dict:
    splits = jax.random.split(jax.random.key(seed), 7)
    return {
        "inputs": scatter_about(splits[0], (SEQS, LENGTH, R), 1.0, 6.0, ((0, 4), (1, 8)), jnp.float32),
        "out_cotangent": scatter_about(splits[1], (SEQS, LENGTH, R), 1.0, 6.0, ((0, 4), (1, 8)), jnp.float32),
        "skip_cotangent": scatter_about(splits[2], (SEQS, LENGTH, R), 1.0, 6.0, ((0, 4), (1, 8)), jnp.float32),
        "convolution_weight": scatter_about(splits[3], (LAYERS, 2 * R, 2 * G), (2 * R) ** -0.5, 0.25, (), jnp.float32),
        "convolution_bias": scatter_about(splits[4], (LAYERS, 2 * G), 0.5, 3.0, (), jnp.float32),
        "output_weight": scatter_about(splits[5], (LAYERS, G, 2 * R), G ** -0.5, 0.25, (), jnp.float32),
    }


def matmul(left, right):
    return jnp.dot(left, right, precision=lax.Precision.HIGHEST, preferred_element_type=jnp.float32)

def past_rows(values, shift_by):
    zeros = jnp.zeros((shift_by, values.shape[1]), jnp.float32)
    return jnp.concatenate([zeros, values[:-shift_by]], axis=0)

def future_rows(values, shift_by):
    zeros = jnp.zeros((shift_by, values.shape[1]), jnp.float32)
    return jnp.concatenate([values[shift_by:], zeros], axis=0)

def layer_forward_step(values, weight, bias, shift_by):
    earlier = past_rows(values, shift_by)
    joined = jnp.concatenate([earlier, values], axis=1)
    mixed = matmul(joined, weight) + bias
    tanh_part = jnp.tanh(mixed[:, :G])
    sigm_part = jax.nn.sigmoid(mixed[:, G:])
    return (joined, tanh_part, sigm_part, tanh_part * sigm_part)

def layer_backward_step(joined, tanh_part, sigm_part, hidden, weight, out_w, carried_state, skip_cotangent_rows, shift_by):
    outer = jnp.concatenate([carried_state, skip_cotangent_rows], axis=1)
    dhidden = matmul(outer, out_w.T)
    dfilter = dhidden * sigm_part * (1.0 - tanh_part * tanh_part)
    dgate = dhidden * tanh_part * sigm_part * (1.0 - sigm_part)
    dmixed = jnp.concatenate([dfilter, dgate], axis=1)
    out_t = matmul(outer.T, hidden)
    conv_g = matmul(joined.T, dmixed)
    bias_g = lax.optimization_barrier(jnp.sum(dmixed, axis=0))
    back = matmul(dmixed, weight.T)
    new_carried = carried_state + back[:, R:] + future_rows(back[:, :R], shift_by)
    return (new_carried, conv_g, out_t, bias_g)

def one_sequence(packed, convolution_weight, convolution_bias, output_weight):
    start_row, output_cotangent_rows, skip_cotangent_rows = (packed[0], packed[1], packed[2])
    first_joined, first_tanh, first_sigmoid, first_hidden = layer_forward_step(start_row, convolution_weight[0], convolution_bias[0], FIRST_DILATION)
    second_layer = start_row + matmul(first_hidden, output_weight[0][:, :R])
    second_joined, second_tanh, second_sigmoid, second_hidden = layer_forward_step(second_layer, convolution_weight[1], convolution_bias[1], SECOND_DILATION)
    carried_state, second_conv_output, second_output, second_bias = layer_backward_step(second_joined, second_tanh, second_sigmoid, second_hidden, convolution_weight[1], output_weight[1], output_cotangent_rows, skip_cotangent_rows, SECOND_DILATION)
    carried_state, first_conv_output, first_output, first_bias = layer_backward_step(first_joined, first_tanh, first_sigmoid, first_hidden, convolution_weight[0], output_weight[0], carried_state, skip_cotangent_rows, FIRST_DILATION)
    return (carried_state, jnp.concatenate([first_conv_output, second_conv_output], axis=0), jnp.concatenate([first_output, second_output], axis=0), jnp.concatenate([first_bias, second_bias], axis=0))

def reference(inputs, out_cotangent, skip_cotangent, convolution_weight, convolution_bias, output_weight):
    packed = jnp.stack([inputs, out_cotangent, skip_cotangent], axis=1)
    grads, conv_all, out_all, bias_all = lax.map(lambda item: one_sequence(item, convolution_weight, convolution_bias, output_weight), packed)
    factor = 1.0 / math.sqrt(SEQS * LENGTH)
    return (grads, lax.optimization_barrier(jnp.sum(conv_all, axis=0)) * factor, lax.optimization_barrier(jnp.sum(out_all, axis=0)) * factor, lax.optimization_barrier(jnp.sum(bias_all, axis=0)) * factor)
```

```python
import functools
import math

import jax
import jax.numpy as jnp
from jax import lax
from jax.experimental import pallas as pl
from jax.experimental.pallas import tpu as pltpu
from jax.sharding import PartitionSpec as P

F32, BF16 = jnp.float32, jnp.bfloat16
NN = (((1,), (0,)), ((), ()))
NT = (((1,), (1,)), ((), ()))
TILE = 256
X_FIRST = (896, 1152)


def split(value):
    high = value.astype(BF16)
    return high, (value - high.astype(F32)).astype(BF16)


def dot3(left, right, dims):
    product = functools.partial(lax.dot_general, dimension_numbers=dims, preferred_element_type=F32)
    (lh, ll), (rh, rl) = left, right
    return (product(ll, rh) + product(lh, rl)) + product(lh, rh)


def kernel(n_seq, n_dp, fused, factor, *refs):
    refs = list(refs)
    x, c2, sk, cw, cb, ow = refs[:6]
    ig, conv_o, out_o, bias_o = refs[6:10]
    (wch, wcl, woh, wol, jh, jl, jth, jtl, hh, hl, fa, ga, oth, otl, dhs, dzh, dzl,
     x2, x2p, tail, q2, q2r, q1, q1r, c1, bsum, ssem, rsem) = refs[10:38]
    if fused:
        grad, rc, rx, ry, rz = refs[38:]
    rows, chan = x.shape[1], x.shape[2]
    half = rows // 2
    gate = ow.shape[1]
    width = 3 * gate + 128
    A, B = pl.ds(0, half), pl.ds(half, half)

    seq, dp = lax.axis_index("seq"), lax.axis_index("dp")
    has_next, has_prev = seq < n_seq - 1, seq > 0
    nxt, prv = lax.rem(seq + 1, n_seq), lax.rem(seq + n_seq - 1, n_seq)
    me_z, me_y, me_x, me_c = seq // 2, seq % 2, dp // 2, dp % 2

    barrier = pltpu.get_barrier_semaphore()
    greet = [(nxt, dp), (prv, dp)]
    if fused:
        greet += [(seq, 2 * me_x + 1 - me_c), (seq, 2 * (1 - me_x) + me_c), (2 * me_z + 1 - me_y, dp)]
        greet += [(lax.rem(seq + 2 * k, n_seq), dp) for k in range(1, n_seq // 2)]
    for s, d in greet:
        pl.semaphore_signal(barrier, inc=1, device_id=(s, d), device_id_type=pl.DeviceIdType.MESH)
    pl.semaphore_wait(barrier, len(greet))

    def remote(src, dst, send, recv, s, d):
        return pltpu.make_async_remote_copy(
            src_ref=src, dst_ref=dst, send_sem=ssem.at[send], recv_sem=rsem.at[recv],
            device_id=(s, d), device_id_type=pl.DeviceIdType.MESH)

    t_copy = remote(x.at[0, B], tail, 0, 0, nxt, dp)
    x2_copy = [remote(x2.at[r], x2p.at[r], 1 + i, 1 + i, nxt, dp) for i, r in enumerate((A, B))]
    q2_copy = [remote(q2.at[r], q2r.at[r], 3 + i, 3 + i, prv, dp) for i, r in enumerate((A, B))]
    q1_copy = remote(q1.at[A], q1r, 5, 5, prv, dp)

    pl.when(has_next)(t_copy.start)

    @pl.when(jnp.logical_not(has_prev))
    def _():
        tail[...] = jnp.zeros_like(tail)
        x2p[...] = jnp.zeros_like(x2p)

    @pl.when(jnp.logical_not(has_next))
    def _():
        q2r[...] = jnp.zeros_like(q2r)
        q1r[...] = jnp.zeros_like(q1r)

    def split_weights(l):
        wch[l], wcl[l] = split(cw[l])
        woh[l], wol[l] = split(ow[l])

    def put_joined(l, r, c0, value):
        cols = pl.ds(c0, chan)
        jh[l, r, cols], jl[l, r, cols] = split(value)
        jth[l, cols, r], jtl[l, cols, r] = split(value.T)

    def put_outer(l, r, c0, value):
        cols = pl.ds(c0, chan)
        oth[l, cols, r], otl[l, cols, r] = split(value.T)

    def forward(l, r):
        joined = (jh[l, r, :], jl[l, r, :])
        for n in range(gate // TILE):
            cols, gcols = pl.ds(n * TILE, TILE), pl.ds(gate + n * TILE, TILE)
            f = dot3(joined, (wch[l, :, cols], wcl[l, :, cols]), NN) + cb[l:l + 1, cols]
            g = dot3(joined, (wch[l, :, gcols], wcl[l, :, gcols]), NN) + cb[l:l + 1, gcols]
            t, s = jnp.tanh(f), jax.nn.sigmoid(g)
            h = t * s
            fa[l, r, cols] = s * (1.0 - t * t)
            ga[l, r, cols] = h * (1.0 - s)
            hh[l, r, cols], hl[l, r, cols] = split(h)

    def second_input(r):
        out = pl.ds(0, chan)
        value = x[0, r, :] + dot3((hh[0, r, :], hl[0, r, :]), (woh[0, :, out], wol[0, :, out]), NN)
        x2[r, :] = value
        return value

    def dmixed(l, r, dh, i):
        df, dg = dh * fa[l, r, :], dh * ga[l, r, :]
        dzh[l, r, :gate], dzl[l, r, :gate] = split(df)
        dzh[l, r, gate:], dzl[l, r, gate:] = split(dg)
        bsum[l, i:i + 1, :gate] = jnp.sum(df, axis=0, keepdims=True)
        bsum[l, i:i + 1, gate:] = jnp.sum(dg, axis=0, keepdims=True)

    def back(l, r, c0):
        taps = pl.ds(c0, chan)
        return dot3((dzh[l, r, :], dzl[l, r, :]), (wch[l, taps, :], wcl[l, taps, :]), NT)

    def put_grad(l, kind, c0, value):
        if not fused:
            (conv_o if kind == 0 else out_o)[l, :, c0:c0 + TILE] = value
            return
        c0 += kind * 2 * gate
        block = value.shape[0] // 16
        for j in range(16):
            grad[l, j % 2, j // 2 % 2, j // 4 % 2, j // 8, :, c0:c0 + TILE] = value[j * block:(j + 1) * block]

    def out_grads(l):
        for n in range(gate // TILE):
            cols = pl.ds(n * TILE, TILE)
            put_grad(l, 1, n * TILE, dot3((oth[l], otl[l]), (hh[l, :, cols], hl[l, :, cols]), NN))

    def conv_grads(l):
        for n in range(2 * gate // TILE):
            cols = pl.ds(n * TILE, TILE)
            put_grad(l, 0, n * TILE, dot3((jth[l], jtl[l]), (dzh[l, :, cols], dzl[l, :, cols]), NN))
        total = bsum[l, 0:1, :] + bsum[l, 1:2, :]
        if not fused:
            bias_o[l:l + 1, :] = total
            return
        piece = 2 * gate // 16
        for j in range(16):
            spot = (l, j % 2, j // 2 % 2, j // 4 % 2, j // 8)
            grad[spot + (slice(None), slice(3 * gate, width))] = jnp.zeros((grad.shape[5], 128), F32)
            grad[spot + (slice(0, 1), slice(3 * gate, 3 * gate + piece))] = total[:, j * piece:(j + 1) * piece]

    copies = []

    def sums(l):
        base = 6 + 9 * l
        ax, by = pl.ds(0, X_FIRST[l]), pl.ds(X_FIRST[l], width - X_FIRST[l])
        other_c = (seq, 2 * me_x + 1 - me_c)
        other_x = (seq, 2 * (1 - me_x) + me_c)
        other_y = (2 * me_z + 1 - me_y, dp)
        own = grad.at[l, me_c]

        def go(src, dst, k, peer):
            copy = remote(src, dst, base + k, base + k, *peer)
            copy.start()
            copies.append(copy)
            return copy

        core = go(grad.at[l, 1 - me_c], rc.at[l], 0, other_c)
        yield
        core.wait_recv()
        own[...] += rc[l]
        xa = go(own.at[1 - me_x, :, :, :, ax], rx.at[l, :, :, :, ax], 1, other_x)
        yb = go(own.at[:, 1 - me_y, :, :, by], ry.at[l, :, :, :, by], 2, other_y)
        yield
        xa.wait_recv()
        own[me_x, :, :, :, ax] += rx[l, :, :, :, ax]
        ya = go(own.at[me_x, 1 - me_y, :, :, ax], ry.at[l, 0, :, :, ax], 3, other_y)
        yb.wait_recv()
        own[:, me_y, :, :, by] += ry[l, :, :, :, by]
        xb = go(own.at[1 - me_x, me_y, :, :, by], rx.at[l, 0, :, :, by], 4, other_x)
        yield
        ya.wait_recv()
        own[me_x, me_y, :, :, ax] += ry[l, 0, :, :, ax]
        xb.wait_recv()
        own[me_x, me_y, :, :, by] += rx[l, 0, :, :, by]
        to_owner = []
        for low in range(2):
            owner = 2 * l + low
            copy = remote(own.at[me_x, me_y, low], rz.at[l, me_z], base + 5 + low, base + 5 + me_z, 2 * owner + me_y, dp)
            pl.when(me_z != owner)(copy.start)
            to_owner.append((owner, copy))
        yield

        @pl.when(me_z // 2 == l)
        def _():
            rz[l, me_z] = own[me_x, me_y, me_z % 2]
            for z in range(4):
                landed = remote(rz.at[l, z], rz.at[l, z], base + 5, base + 5 + z, seq, dp)
                pl.when(me_z != z)(landed.wait_recv)
            total = ((rz[l, 0] + rz[l, 1]) + (rz[l, 2] + rz[l, 3])) * factor
            conv_o[...] = total[:, :2 * gate]
            out_o[...] = total[:, 2 * gate:3 * gate]
            bias_o[...] = total[:8, 3 * gate:]

        for owner, copy in to_owner:
            pl.when(me_z != owner)(copy.wait_send)
        yield

    split_weights(0)
    put_joined(0, B, 0, x[0, A, :])
    put_joined(0, A, chan, x[0, A, :])
    put_joined(0, B, chan, x[0, B, :])
    forward(0, B)
    second_b = second_input(B)
    pl.when(has_next)(x2_copy[1].start)
    put_joined(1, B, chan, second_b)
    split_weights(1)
    for r in (A, B):
        for l in range(2):
            put_outer(l, r, chan, sk[0, r, :])
        put_outer(1, r, 0, c2[0, r, :])
    late, early = pl.ds(chan, chan), pl.ds(0, chan)
    for r in (A, B):
        skip = split(sk[0, r, :])
        dhs[0, r, :] = dot3(skip, (woh[0, :, late], wol[0, :, late]), NT)
        dhs[1, r, :] = dot3(skip, (woh[1, :, late], wol[1, :, late]), NT) + dot3(
            split(c2[0, r, :]), (woh[1, :, early], wol[1, :, early]), NT)
    pl.when(has_prev)(t_copy.wait_recv)
    put_joined(0, A, 0, tail[...])
    forward(0, A)
    second_a = second_input(A)
    pl.when(has_next)(x2_copy[0].start)
    put_joined(1, A, chan, second_a)
    for i in (1, 0):
        r = (A, B)[i]
        pl.when(has_prev)(x2_copy[i].wait_recv)
        put_joined(1, r, 0, x2p[r, :])
        forward(1, r)
        dmixed(1, r, dhs[1, r, :], i)
        q2[r, :] = back(1, r, 0)
        pl.when(has_prev)(q2_copy[i].start)
    out_grads(1)
    conv_grads(1)
    if fused:
        second_sums = sums(1)
        next(second_sums)
    out_later = []
    for i in (1, 0):
        r = (A, B)[i]
        c1[r, :] = c2[0, r, :] + back(1, r, chan)
    if fused:
        next(second_sums)
    for i in (1, 0):
        r = (A, B)[i]
        pl.when(has_next)(q2_copy[i].wait_recv)
        carried = c1[r, :] + q2r[r, :]
        c1[r, :] = carried
        put_outer(0, r, 0, carried)
        dmixed(0, r, dhs[0, r, :] + dot3(split(carried), (woh[0, :, early], wol[0, :, early]), NT), i)
        q1[r, :] = back(0, r, 0)
        if i == 0:
            pl.when(has_prev)(q1_copy.start)
    out_grads(0)
    conv_grads(0)
    if fused:
        first_sums = sums(0)
        next(first_sums)
        next(second_sums)
    ig[0, A, :] = c1[A, :] + back(0, A, chan) + q1[B, :]
    if fused:
        next(first_sums)
    inner = c1[B, :] + back(0, B, chan)
    pl.when(has_next)(q1_copy.wait_recv)
    ig[0, B, :] = inner + q1r[...]
    if fused:
        next(second_sums)
        next(first_sums)
        next(first_sums)
        next(second_sums)
        next(first_sums)
    pl.when(has_next)(t_copy.wait_send)
    for i in range(2):
        pl.when(has_next)(x2_copy[i].wait_send)
        pl.when(has_prev)(q2_copy[i].wait_send)
    pl.when(has_prev)(q1_copy.wait_send)
    for copy in copies:
        copy.wait_send()


def local(n_seq, n_dp, *args):
    inputs, _, _, convolution_weight, _, output_weight = args
    _, rows, chan = inputs.shape
    half = rows // 2
    gate = output_weight.shape[1]
    fused = (n_seq, n_dp) == (8, 4)
    factor = 1.0 / math.sqrt(rows * n_seq * n_dp)
    block = 2 * (2 * chan) // (n_seq * n_dp)
    width = 3 * gate + 128
    vmem, sds = pltpu.VMEM, jax.ShapeDtypeStruct
    if fused:
        grads = [sds((block, 2 * gate), F32), sds((block, gate), F32), sds((8, 128), F32)]
    else:
        grads = [sds((2, 2 * chan, 2 * gate), F32), sds((2, 2 * chan, gate), F32), sds((2, 2 * gate), F32)]
    pair = lambda *shape: [vmem(shape, BF16)] * 2
    scratch = [
        *pair(2, 2 * chan, 2 * gate), *pair(2, gate, 2 * chan),
        *pair(2, rows, 2 * chan), *pair(2, 2 * chan, rows), *pair(2, rows, gate),
        vmem((2, rows, gate), F32), vmem((2, rows, gate), F32),
        *pair(2, 2 * chan, rows), vmem((2, rows, gate), F32), *pair(2, rows, 2 * gate),
        vmem((rows, chan), F32), vmem((rows, chan), F32), vmem((half, chan), F32),
        vmem((rows, chan), F32), vmem((rows, chan), F32), vmem((rows, chan), F32),
        vmem((half, chan), F32), vmem((rows, chan), F32), vmem((2, 8, 2 * gate), F32),
        pltpu.SemaphoreType.DMA((24,)), pltpu.SemaphoreType.DMA((24,)),
    ]
    if fused:
        scratch += [
            vmem((2, 2, 2, 2, 2, block, width), F32), vmem((2, 2, 2, 2, block, width), F32),
            vmem((2, 2, 2, block, width), F32), vmem((2, 2, 2, block, width), F32),
            vmem((2, 4, block, width), F32),
        ]
    spec = pl.BlockSpec(memory_space=pltpu.VMEM)
    input_grad, conv, out, bias = pl.pallas_call(
        functools.partial(kernel, n_seq, n_dp, fused, factor),
        out_shape=[sds(inputs.shape, F32)] + grads,
        in_specs=[spec] * 6,
        out_specs=[spec] * 4,
        scratch_shapes=scratch,
        compiler_params=pltpu.CompilerParams(
            collective_id=0, has_side_effects=True, vmem_limit_bytes=60 * 1024 * 1024),
    )(*args)
    if fused:
        return input_grad, conv, out, bias[0, : 4 * gate // (n_seq * n_dp)]

    def scattered(terms):
        terms = terms.reshape((-1,) + terms.shape[2:]) * factor
        part = lax.psum_scatter(terms, "seq", scatter_dimension=0, tiled=True)
        return lax.psum_scatter(part, "dp", scatter_dimension=0, tiled=True)

    return input_grad, scattered(conv), scattered(out), scattered(bias)


def solution(mesh):
    return jax.shard_map(
        functools.partial(local, mesh.shape["seq"], mesh.shape["dp"]),
        mesh=mesh,
        in_specs=(P("dp", "seq", None),) * 3 + (P(), P(), P()),
        out_specs=(P("dp", "seq", None), P(("seq", "dp"), None), P(("seq", "dp"), None), P(("seq", "dp"))),
        check_vma=False,
    )
```

```python
import functools
import math

import jax
import jax.numpy as jnp
from jax import lax
from jax.experimental import pallas as pl
from jax.experimental.pallas import tpu as pltpu
from jax.sharding import PartitionSpec as P

F32, BF16 = jnp.float32, jnp.bfloat16
NN = (((1,), (0,)), ((), ()))
NT = (((1,), (1,)), ((), ()))
TILE = 256


def split(value):
    high = value.astype(BF16)
    return high, (value - high.astype(F32)).astype(BF16)


def dot3(left, right, dims):
    product = functools.partial(lax.dot_general, dimension_numbers=dims, preferred_element_type=F32)
    (lh, ll), (rh, rl) = left, right
    return (product(ll, rh) + product(lh, rl)) + product(lh, rh)


def kernel(n_seq, n_dp, fused, factor, *refs):
    refs = list(refs)
    x, c2_in, sk_in, cw_in, cb, ow_in = refs[:6]
    ig, conv_o, out_o, bias_o = refs[6:10]
    (wch, wcl, woh, wol, jh, jl, jth, jtl, hh, hl, fa, ga, oth, otl, dhs, dzh, dzl,
     x2, x2p, tail, q2, q2r, q1, q1r, c1, bsum, c2, sk, cw, ow, ssem, rsem, lsem) = refs[10:43]
    if fused:
        grad, rc, r1, r2, rz, rf = refs[43:]
    rows, chan = x.shape[1], x.shape[2]
    half = rows // 2
    gate = ow_in.shape[1]
    width = 3 * gate + 128
    A, B = pl.ds(0, half), pl.ds(half, half)

    seq, dp = lax.axis_index("seq"), lax.axis_index("dp")
    has_next, has_prev = seq < n_seq - 1, seq > 0
    nxt, prv = lax.rem(seq + 1, n_seq), lax.rem(seq + n_seq - 1, n_seq)
    me_z, me_y, me_x, me_c = seq // 2, seq % 2, dp // 2, dp % 2

    fetches = {}
    for i, (name, src, dst) in enumerate((
        ("cw0", cw_in.at[0], cw.at[0]), ("ow0", ow_in.at[0], ow.at[0]), ("sk", sk_in, sk),
        ("c2", c2_in, c2), ("ow1", ow_in.at[1], ow.at[1]), ("cw1", cw_in.at[1], cw.at[1]))):
        fetches[name] = pltpu.make_async_copy(src, dst, lsem.at[i])
        fetches[name].start()

    barrier = pltpu.get_barrier_semaphore()
    greet = [(nxt, dp), (prv, dp)]
    if fused:
        greet += [(seq, 2 * me_x + 1 - me_c), (seq, 2 * (1 - me_x) + me_c), (2 * me_z + 1 - me_y, dp)]
        greet += [(lax.rem(seq + 2 * k, n_seq), dp) for k in range(1, n_seq // 2)]
    for s, d in greet:
        pl.semaphore_signal(barrier, inc=1, device_id=(s, d), device_id_type=pl.DeviceIdType.MESH)
    pl.semaphore_wait(barrier, len(greet))

    def remote(src, dst, send, recv, s, d):
        return pltpu.make_async_remote_copy(
            src_ref=src, dst_ref=dst, send_sem=ssem.at[send], recv_sem=rsem.at[recv],
            device_id=(s, d), device_id_type=pl.DeviceIdType.MESH)

    t_copy = remote(x.at[0, B], tail, 0, 0, nxt, dp)
    x2_copy = [remote(x2.at[r], x2p.at[r], 1 + i, 1 + i, nxt, dp) for i, r in enumerate((A, B))]
    q2_copy = [remote(q2.at[r], q2r.at[r], 3 + i, 3 + i, prv, dp) for i, r in enumerate((A, B))]
    q1_copy = remote(q1.at[A], q1r, 5, 5, prv, dp)

    pl.when(has_next)(t_copy.start)

    @pl.when(jnp.logical_not(has_prev))
    def _():
        tail[...] = jnp.zeros_like(tail)
        x2p[...] = jnp.zeros_like(x2p)

    @pl.when(jnp.logical_not(has_next))
    def _():
        q2r[...] = jnp.zeros_like(q2r)
        q1r[...] = jnp.zeros_like(q1r)

    def split_conv(l):
        fetches["cw%d" % l].wait()
        wch[l], wcl[l] = split(cw[l])

    def split_out(l):
        fetches["ow%d" % l].wait()
        woh[l], wol[l] = split(ow[l])

    def put_joined(l, r, c0, value):
        cols = pl.ds(c0, chan)
        jh[l, r, cols], jl[l, r, cols] = split(value)
        jth[l, cols, r], jtl[l, cols, r] = split(value.T)

    def put_outer(l, r, c0, value):
        cols = pl.ds(c0, chan)
        oth[l, cols, r], otl[l, cols, r] = split(value.T)

    def forward(l, r):
        joined = (jh[l, r, :], jl[l, r, :])
        for n in range(gate // TILE):
            cols, gcols = pl.ds(n * TILE, TILE), pl.ds(gate + n * TILE, TILE)
            f = dot3(joined, (wch[l, :, cols], wcl[l, :, cols]), NN) + cb[l:l + 1, cols]
            g = dot3(joined, (wch[l, :, gcols], wcl[l, :, gcols]), NN) + cb[l:l + 1, gcols]
            t, s = jnp.tanh(f), jax.nn.sigmoid(g)
            h = t * s
            fa[l, r, cols] = s * (1.0 - t * t)
            ga[l, r, cols] = h * (1.0 - s)
            hh[l, r, cols], hl[l, r, cols] = split(h)

    def second_input(r):
        out = pl.ds(0, chan)
        value = x[0, r, :] + dot3((hh[0, r, :], hl[0, r, :]), (woh[0, :, out], wol[0, :, out]), NN)
        x2[r, :] = value
        return value

    def dmixed(l, r, dh, i):
        df, dg = dh * fa[l, r, :], dh * ga[l, r, :]
        dzh[l, r, :gate], dzl[l, r, :gate] = split(df)
        dzh[l, r, gate:], dzl[l, r, gate:] = split(dg)
        bsum[l, i:i + 1, :gate] = jnp.sum(df, axis=0, keepdims=True)
        bsum[l, i:i + 1, gate:] = jnp.sum(dg, axis=0, keepdims=True)

    def back(l, r, c0):
        taps = pl.ds(c0, chan)
        return dot3((dzh[l, r, :], dzl[l, r, :]), (wch[l, taps, :], wcl[l, taps, :]), NT)

    def put_grad(l, kind, c0, value):
        if not fused:
            (conv_o if kind == 0 else out_o)[l, :, c0:c0 + TILE] = value
            return
        c0 += kind * 2 * gate
        block = value.shape[0] // 16
        for j in range(16):
            grad[l, j % 2, j // 2 % 2, j // 4 % 2, j // 8, :, c0:c0 + TILE] = value[j * block:(j + 1) * block]

    def grad_tile(l, k):
        if k < n_out:
            cols = pl.ds(k * TILE, TILE)
            put_grad(l, 1, k * TILE, dot3((oth[l], otl[l]), (hh[l, :, cols], hl[l, :, cols]), NN))
            return
        c0 = (k - n_out) * TILE
        cols = pl.ds(c0, TILE)
        put_grad(l, 0, c0, dot3((jth[l], jtl[l]), (dzh[l, :, cols], dzl[l, :, cols]), NN))

    def bias_grad(l):
        total = bsum[l, 0:1, :] + bsum[l, 1:2, :]
        if not fused:
            bias_o[l:l + 1, :] = total
            return
        piece = 2 * gate // 16
        for j in range(16):
            spot = (l, j % 2, j // 2 % 2, j // 4 % 2, j // 8)
            grad[spot + (slice(None), slice(3 * gate, width))] = jnp.zeros((grad.shape[5], 128), F32)
            grad[spot + (slice(0, 1), slice(3 * gate, 3 * gate + piece))] = total[:, j * piece:(j + 1) * piece]

    n_out, tiles = gate // TILE, 3 * gate // TILE
    copies = []

    def go(src, dst, k, peer):
        copy = remote(src, dst, k, k, *peer)
        copy.start()
        copies.append(copy)
        return copy

    def chunk(l, k):
        base = 6 + 6 * (tiles * l + k)
        if k < n_out:
            c0, size = 2 * gate + k * TILE, TILE
        else:
            c0, size = (k - n_out) * TILE, TILE
        if k == n_out - 1:
            size += 128
        cols = pl.ds(c0, size)
        x_first = k % 2 == 0
        other_c = (seq, 2 * me_x + 1 - me_c)
        other_x = (seq, 2 * (1 - me_x) + me_c)
        other_y = (2 * me_z + 1 - me_y, dp)
        own = grad.at[l, me_c]
        place = me_z if l == 0 else 3 - me_z
        low = lambda p: p if l == 0 else 1 - p
        at_place = lambda p: (2 * (p if l == 0 else 3 - p) + me_y, dp)

        if k == n_out - 1:
            bias_grad(l)
        grad_tile(l, k)
        core = go(grad.at[l, 1 - me_c, :, :, :, :, cols], rc.at[l, :, :, :, :, cols], base, other_c)
        yield
        core.wait_recv()
        own[:, :, :, :, cols] += rc[l, :, :, :, :, cols]
        if x_first:
            first = go(own.at[1 - me_x, :, :, :, cols], r1.at[l, :, :, :, cols], base + 1, other_x)
        else:
            first = go(own.at[:, 1 - me_y, :, :, cols], r1.at[l, :, :, :, cols], base + 1, other_y)
        yield
        first.wait_recv()
        if x_first:
            own[me_x, :, :, :, cols] += r1[l, :, :, :, cols]
            second = go(own.at[me_x, 1 - me_y, :, :, cols], r2.at[l, :, :, cols], base + 2, other_y)
        else:
            own[:, me_y, :, :, cols] += r1[l, :, :, :, cols]
            second = go(own.at[1 - me_x, me_y, :, :, cols], r2.at[l, :, :, cols], base + 2, other_x)
        yield
        second.wait_recv()
        mine = own.at[me_x, me_y]
        mine[:, :, cols] += r2[l, :, :, cols]
        both = [remote(mine.at[:, :, cols], rz.at[l, :, :, cols], base + 3, base + 3, *at_place(p)) for p in (1, 2)]
        up = remote(mine.at[low(0), :, cols], rf.at[l, :, cols], base + 3, base + 4, *at_place(0))
        down = remote(mine.at[low(1), :, cols], rf.at[l, :, cols], base + 3, base + 4, *at_place(1))
        pl.when(place == 3)(both[1].start)
        pl.when(place == 0)(down.start)
        yield

        @pl.when(place == 2)
        def _():
            both[1].wait_recv()
            mine[:, :, cols] += rz[l, :, :, cols]
            both[0].start()

        yield

        def finish(p):
            total = (mine[low(p), :, cols] + rf[l, :, cols]) * factor
            if k < n_out:
                out_o[:, k * TILE:(k + 1) * TILE] = total[:, :TILE]
            else:
                conv_o[:, c0:c0 + TILE] = total
            if size > TILE:
                bias_o[...] = total[:8, TILE:]

        @pl.when(place == 1)
        def _():
            both[0].wait_recv()
            mine[:, :, cols] += rz[l, :, :, cols]
            up.start()
            down.wait_recv()
            finish(1)

        yield

        @pl.when(place == 0)
        def _():
            up.wait_recv()
            finish(0)
            down.wait_send()

        pl.when(place == 1)(up.wait_send)
        pl.when(place == 2)(both[0].wait_send)
        pl.when(place == 3)(both[1].wait_send)
        yield

    chunks = [[chunk(l, k) for k in range(tiles)] for l in range(2)]

    def advance(l, *which):
        if fused:
            for k in which or range(tiles):
                next(chunks[l][k])

    def all_grads(l):
        if fused:
            return
        for k in range(tiles):
            grad_tile(l, k)
        bias_grad(l)

    put_joined(0, B, 0, x[0, A, :])
    put_joined(0, B, chan, x[0, B, :])
    split_conv(0)
    forward(0, B)
    split_out(0)
    second_b = second_input(B)
    pl.when(has_next)(x2_copy[1].start)
    put_joined(0, A, chan, x[0, A, :])
    put_joined(1, B, chan, second_b)
    late, early = pl.ds(chan, chan), pl.ds(0, chan)
    fetches["sk"].wait()
    for r in (A, B):
        for l in range(2):
            put_outer(l, r, chan, sk[0, r, :])
        dhs[0, r, :] = dot3(split(sk[0, r, :]), (woh[0, :, late], wol[0, :, late]), NT)
    pl.when(has_prev)(t_copy.wait_recv)
    put_joined(0, A, 0, tail[...])
    forward(0, A)
    second_a = second_input(A)
    pl.when(has_next)(x2_copy[0].start)
    put_joined(1, A, chan, second_a)
    split_conv(1)
    split_out(1)
    fetches["c2"].wait()
    for r in (B, A):
        put_outer(1, r, 0, c2[0, r, :])
        dhs[1, r, :] = dot3(split(sk[0, r, :]), (woh[1, :, late], wol[1, :, late]), NT) + dot3(
            split(c2[0, r, :]), (woh[1, :, early], wol[1, :, early]), NT)
    for i in (1, 0):
        r = (A, B)[i]
        pl.when(has_prev)(x2_copy[i].wait_recv)
        put_joined(1, r, 0, x2p[r, :])
        forward(1, r)
        dmixed(1, r, dhs[1, r, :], i)
        q2[r, :] = back(1, r, 0)
        pl.when(has_prev)(q2_copy[i].start)
    all_grads(1)
    advance(1)
    for i in (1, 0):
        r = (A, B)[i]
        c1[r, :] = c2[0, r, :] + back(1, r, chan)
    advance(1)
    for i in (1, 0):
        r = (A, B)[i]
        pl.when(has_next)(q2_copy[i].wait_recv)
        carried = c1[r, :] + q2r[r, :]
        c1[r, :] = carried
        dmixed(0, r, dhs[0, r, :] + dot3(split(carried), (woh[0, :, early], wol[0, :, early]), NT), i)
        q1[r, :] = back(0, r, 0)
        if i == 0:
            pl.when(has_prev)(q1_copy.start)
        put_outer(0, r, 0, carried)
    all_grads(0)
    for k in range(tiles):
        advance(0, k)
        advance(1, k)
    advance(0)
    advance(1)
    ig[0, A, :] = c1[A, :] + back(0, A, chan) + q1[B, :]
    inner = c1[B, :] + back(0, B, chan)
    pl.when(has_next)(q1_copy.wait_recv)
    ig[0, B, :] = inner + q1r[...]
    for stage in range(3):
        for k in range(tiles):
            advance(0, k)
            advance(1, k)
    advance(0)
    advance(0)
    pl.when(has_next)(t_copy.wait_send)
    for i in range(2):
        pl.when(has_next)(x2_copy[i].wait_send)
        pl.when(has_prev)(q2_copy[i].wait_send)
    pl.when(has_prev)(q1_copy.wait_send)
    for copy in copies:
        copy.wait_send()


def hand_on(a, b, c, bias, a_out, b_out, c_out, bias_out, sems):
    moves = [pltpu.make_async_copy(*pair, sems.at[i]) for i, pair in enumerate(((a, a_out), (b, b_out), (c, c_out)))]
    for move in moves:
        move.start()
    bias_out[...] = bias[0, : bias_out.shape[0]]
    for move in moves:
        move.wait()


def local(n_seq, n_dp, *args):
    inputs, _, _, convolution_weight, _, output_weight = args
    _, rows, chan = inputs.shape
    half = rows // 2
    gate = output_weight.shape[1]
    fused = (n_seq, n_dp) == (8, 4)
    factor = 1.0 / math.sqrt(rows * n_seq * n_dp)
    block = 2 * (2 * chan) // (n_seq * n_dp)
    width = 3 * gate + 128
    vmem, sds = pltpu.VMEM, jax.ShapeDtypeStruct
    if fused:
        grads = [sds((block, 2 * gate), F32), sds((block, gate), F32), sds((8, 128), F32)]
    else:
        grads = [sds((2, 2 * chan, 2 * gate), F32), sds((2, 2 * chan, gate), F32), sds((2, 2 * gate), F32)]
    pair = lambda *shape: [vmem(shape, BF16)] * 2
    scratch = [
        *pair(2, 2 * chan, 2 * gate), *pair(2, gate, 2 * chan),
        *pair(2, rows, 2 * chan), *pair(2, 2 * chan, rows), *pair(2, rows, gate),
        vmem((2, rows, gate), F32), vmem((2, rows, gate), F32),
        *pair(2, 2 * chan, rows), vmem((2, rows, gate), F32), *pair(2, rows, 2 * gate),
        vmem((rows, chan), F32), vmem((rows, chan), F32), vmem((half, chan), F32),
        vmem((rows, chan), F32), vmem((rows, chan), F32), vmem((rows, chan), F32),
        vmem((half, chan), F32), vmem((rows, chan), F32), vmem((2, 8, 2 * gate), F32),
        vmem(inputs.shape, F32), vmem(inputs.shape, F32),
        vmem(convolution_weight.shape, F32), vmem(output_weight.shape, F32),
        pltpu.SemaphoreType.DMA((6 + 36 * gate // TILE,)), pltpu.SemaphoreType.DMA((6 + 36 * gate // TILE,)),
        pltpu.SemaphoreType.DMA((6,)),
    ]
    if fused:
        scratch += [
            vmem((2, 2, 2, 2, 2, block, width), F32), vmem((2, 2, 2, 2, block, width), F32),
            vmem((2, 2, 2, block, width), F32), vmem((2, 2, block, width), F32),
            vmem((2, 2, block, width), F32), vmem((2, block, width), F32),
        ]
    spec, anywhere = pl.BlockSpec(memory_space=pltpu.VMEM), pl.BlockSpec(memory_space=pl.ANY)
    input_grad, conv, out, bias = pl.pallas_call(
        functools.partial(kernel, n_seq, n_dp, fused, factor),
        out_shape=[sds(inputs.shape, F32)] + grads,
        in_specs=[spec, anywhere, anywhere, anywhere, spec, anywhere],
        out_specs=[spec] * 4,
        scratch_shapes=scratch,
        compiler_params=pltpu.CompilerParams(
            collective_id=0, has_side_effects=True, vmem_limit_bytes=60 * 1024 * 1024),
    )(*args)
    if fused:
        piece = 4 * gate // (n_seq * n_dp)
        return pl.pallas_call(
            hand_on,
            out_shape=[sds(inputs.shape, F32), *grads[:2], sds((piece,), F32)],
            in_specs=[anywhere] * 3 + [spec],
            out_specs=[anywhere] * 3 + [spec],
            scratch_shapes=[pltpu.SemaphoreType.DMA((3,))],
        )(input_grad, conv, out, bias)

    def scattered(terms):
        terms = terms.reshape((-1,) + terms.shape[2:]) * factor
        part = lax.psum_scatter(terms, "seq", scatter_dimension=0, tiled=True)
        return lax.psum_scatter(part, "dp", scatter_dimension=0, tiled=True)

    return input_grad, scattered(conv), scattered(out), scattered(bias)


def solution(mesh):
    return jax.shard_map(
        functools.partial(local, mesh.shape["seq"], mesh.shape["dp"]),
        mesh=mesh,
        in_specs=(P("dp", "seq", None),) * 3 + (P(), P(), P()),
        out_specs=(P("dp", "seq", None), P(("seq", "dp"), None), P(("seq", "dp"), None), P(("seq", "dp"))),
        check_vma=False,
    )
```

```python
import functools
import math

import jax
import jax.numpy as jnp
from jax import lax
from jax.experimental import pallas as pl
from jax.experimental.pallas import tpu as pltpu
from jax.sharding import PartitionSpec as P

F32, BF16 = jnp.float32, jnp.bfloat16
NN = (((1,), (0,)), ((), ()))
TILE = 256


def split(value):
    high = value.astype(BF16)
    return high, (value - high.astype(F32)).astype(BF16)


def dot3(left, right, dims):
    product = functools.partial(lax.dot_general, dimension_numbers=dims, preferred_element_type=F32)
    (lh, ll), (rh, rl) = left, right
    return (product(ll, rh) + product(lh, rl)) + product(lh, rh)


def kernel(n_seq, n_dp, fused, factor, *refs):
    refs = list(refs)
    x, c2_in, sk_in, cw_in, cb, ow_in = refs[:6]
    ig, conv_o, out_o, bias_o = refs[6:10]
    (wch, wcl, woh, wol, wcth, wctl, woth, wotl, jh, jl, jth, jtl, hh, hl, fa, ga, oth, otl, dhs, dzh, dzl,
     x2, x2p, tail, q2, q2r, q1, q1r, c1, bsum, c2, sk, cw, ow, ssem, rsem, lsem) = refs[10:47]
    if fused:
        grad, rc, r1, r2, rz, rf = refs[47:]
    rows, chan = x.shape[1], x.shape[2]
    half = rows // 2
    gate = ow_in.shape[1]
    width = 3 * gate + 128
    A, B = pl.ds(0, half), pl.ds(half, half)

    seq, dp = lax.axis_index("seq"), lax.axis_index("dp")
    has_next, has_prev = seq < n_seq - 1, seq > 0
    nxt, prv = lax.rem(seq + 1, n_seq), lax.rem(seq + n_seq - 1, n_seq)
    me_z, me_y, me_x, me_c = seq // 2, seq % 2, dp // 2, dp % 2

    fetches = {}
    for i, (name, src, dst) in enumerate((
        ("cw0", cw_in.at[0], cw.at[0]), ("ow0", ow_in.at[0], ow.at[0]), ("sk", sk_in, sk),
        ("c2", c2_in, c2), ("ow1", ow_in.at[1], ow.at[1]), ("cw1", cw_in.at[1], cw.at[1]))):
        fetches[name] = pltpu.make_async_copy(src, dst, lsem.at[i])
        fetches[name].start()

    barrier = pltpu.get_barrier_semaphore()
    greet = [(nxt, dp), (prv, dp)]
    if fused:
        greet += [(seq, 2 * me_x + 1 - me_c), (seq, 2 * (1 - me_x) + me_c), (2 * me_z + 1 - me_y, dp)]
        greet += [(lax.rem(seq + 2 * k, n_seq), dp) for k in range(1, n_seq // 2)]
    for s, d in greet:
        pl.semaphore_signal(barrier, inc=1, device_id=(s, d), device_id_type=pl.DeviceIdType.MESH)
    pl.semaphore_wait(barrier, len(greet))

    def remote(src, dst, send, recv, s, d):
        return pltpu.make_async_remote_copy(
            src_ref=src, dst_ref=dst, send_sem=ssem.at[send], recv_sem=rsem.at[recv],
            device_id=(s, d), device_id_type=pl.DeviceIdType.MESH)

    t_copy = remote(x.at[0, B], tail, 0, 0, nxt, dp)
    x2_copy = [remote(x2.at[r], x2p.at[r], 1 + i, 1 + i, nxt, dp) for i, r in enumerate((A, B))]
    q2_copy = [remote(q2.at[r], q2r.at[r], 3 + i, 3 + i, prv, dp) for i, r in enumerate((A, B))]
    q1_copy = remote(q1.at[A], q1r, 5, 5, prv, dp)

    pl.when(has_next)(t_copy.start)

    @pl.when(jnp.logical_not(has_prev))
    def _():
        tail[...] = jnp.zeros_like(tail)
        x2p[...] = jnp.zeros_like(x2p)

    @pl.when(jnp.logical_not(has_next))
    def _():
        q2r[...] = jnp.zeros_like(q2r)
        q1r[...] = jnp.zeros_like(q1r)

    def split_conv(l):
        fetches["cw%d" % l].wait()
        wch[l], wcl[l] = split(cw[l])

    def split_out(l):
        fetches["ow%d" % l].wait()
        woh[l], wol[l] = split(ow[l])

    def turn_conv(l):
        wcth[l], wctl[l] = split(cw[l].T)

    def turn_out(l):
        woth[l], wotl[l] = split(ow[l].T)

    def put_rows(l, r, c0, value):
        cols = pl.ds(c0, chan)
        jh[l, r, cols], jl[l, r, cols] = split(value)

    def put_turned(l, r, c0, value):
        cols = pl.ds(c0, chan)
        jth[l, cols, r], jtl[l, cols, r] = split(value.T)

    def put_outer(l, r, c0, value):
        cols = pl.ds(c0, chan)
        oth[l, cols, r], otl[l, cols, r] = split(value.T)

    def forward(l, r):
        joined = (jh[l, r, :], jl[l, r, :])
        for n in range(gate // TILE):
            cols, gcols = pl.ds(n * TILE, TILE), pl.ds(gate + n * TILE, TILE)
            f = dot3(joined, (wch[l, :, cols], wcl[l, :, cols]), NN) + cb[l:l + 1, cols]
            g = dot3(joined, (wch[l, :, gcols], wcl[l, :, gcols]), NN) + cb[l:l + 1, gcols]
            t, s = jnp.tanh(f), jax.nn.sigmoid(g)
            h = t * s
            fa[l, r, cols] = s * (1.0 - t * t)
            ga[l, r, cols] = h * (1.0 - s)
            hh[l, r, cols], hl[l, r, cols] = split(h)

    def second_input(r):
        out = pl.ds(0, chan)
        value = x[0, r, :] + dot3((hh[0, r, :], hl[0, r, :]), (woh[0, :, out], wol[0, :, out]), NN)
        x2[r, :] = value
        return value

    def dmixed(l, r, dh, i):
        df, dg = dh * fa[l, r, :], dh * ga[l, r, :]
        dzh[l, r, :gate], dzl[l, r, :gate] = split(df)
        dzh[l, r, gate:], dzl[l, r, gate:] = split(dg)
        bsum[l, i:i + 1, :gate] = jnp.sum(df, axis=0, keepdims=True)
        bsum[l, i:i + 1, gate:] = jnp.sum(dg, axis=0, keepdims=True)

    def back(l, r, c0):
        taps = pl.ds(c0, chan)
        return dot3((dzh[l, r, :], dzl[l, r, :]), (wcth[l, :, taps], wctl[l, :, taps]), NN)

    def put_grad(l, kind, c0, value):
        if not fused:
            (conv_o if kind == 0 else out_o)[l, :, c0:c0 + TILE] = value
            return
        c0 += kind * 2 * gate
        block = value.shape[0] // 16
        for j in range(16):
            grad[l, j % 2, j // 2 % 2, j // 4 % 2, j // 8, :, c0:c0 + TILE] = value[j * block:(j + 1) * block]

    def grad_tile(l, k):
        if k < n_out:
            cols = pl.ds(k * TILE, TILE)
            put_grad(l, 1, k * TILE, dot3((oth[l], otl[l]), (hh[l, :, cols], hl[l, :, cols]), NN))
            return
        c0 = (k - n_out) * TILE
        cols = pl.ds(c0, TILE)
        put_grad(l, 0, c0, dot3((jth[l], jtl[l]), (dzh[l, :, cols], dzl[l, :, cols]), NN))

    def bias_grad(l):
        total = bsum[l, 0:1, :] + bsum[l, 1:2, :]
        if not fused:
            bias_o[l:l + 1, :] = total
            return
        piece = 2 * gate // 16
        for j in range(16):
            spot = (l, j % 2, j // 2 % 2, j // 4 % 2, j // 8)
            grad[spot + (slice(None), slice(3 * gate, width))] = jnp.zeros((grad.shape[5], 128), F32)
            grad[spot + (slice(0, 1), slice(3 * gate, 3 * gate + piece))] = total[:, j * piece:(j + 1) * piece]

    n_out, tiles = gate // TILE, 3 * gate // TILE
    copies = []

    def go(src, dst, k, peer):
        copy = remote(src, dst, k, k, *peer)
        copy.start()
        copies.append(copy)
        return copy

    def chunk(l, k):
        base = 6 + 6 * (tiles * l + k)
        if k < n_out:
            c0, size = 2 * gate + k * TILE, TILE
        else:
            c0, size = (k - n_out) * TILE, TILE
        if k == n_out - 1:
            size += 128
        cols = pl.ds(c0, size)
        x_first = k % 2 == 0
        other_c = (seq, 2 * me_x + 1 - me_c)
        other_x = (seq, 2 * (1 - me_x) + me_c)
        other_y = (2 * me_z + 1 - me_y, dp)
        own = grad.at[l, me_c]
        place = me_z if l == 0 else 3 - me_z
        low = lambda p: p if l == 0 else 1 - p
        at_place = lambda p: (2 * (p if l == 0 else 3 - p) + me_y, dp)

        if k == n_out - 1:
            bias_grad(l)
        grad_tile(l, k)
        core = go(grad.at[l, 1 - me_c, :, :, :, :, cols], rc.at[l, :, :, :, :, cols], base, other_c)
        yield
        core.wait_recv()
        own[:, :, :, :, cols] += rc[l, :, :, :, :, cols]
        if x_first:
            first = go(own.at[1 - me_x, :, :, :, cols], r1.at[l, :, :, :, cols], base + 1, other_x)
        else:
            first = go(own.at[:, 1 - me_y, :, :, cols], r1.at[l, :, :, :, cols], base + 1, other_y)
        yield
        first.wait_recv()
        if x_first:
            own[me_x, :, :, :, cols] += r1[l, :, :, :, cols]
            second = go(own.at[me_x, 1 - me_y, :, :, cols], r2.at[l, :, :, cols], base + 2, other_y)
        else:
            own[:, me_y, :, :, cols] += r1[l, :, :, :, cols]
            second = go(own.at[1 - me_x, me_y, :, :, cols], r2.at[l, :, :, cols], base + 2, other_x)
        yield
        second.wait_recv()
        mine = own.at[me_x, me_y]
        mine[:, :, cols] += r2[l, :, :, cols]
        both = [remote(mine.at[:, :, cols], rz.at[l, :, :, cols], base + 3, base + 3, *at_place(p)) for p in (1, 2)]
        up = remote(mine.at[low(0), :, cols], rf.at[l, :, cols], base + 3, base + 4, *at_place(0))
        down = remote(mine.at[low(1), :, cols], rf.at[l, :, cols], base + 3, base + 4, *at_place(1))
        pl.when(place == 3)(both[1].start)
        pl.when(place == 0)(down.start)
        yield

        @pl.when(place == 2)
        def _():
            both[1].wait_recv()
            mine[:, :, cols] += rz[l, :, :, cols]
            both[0].start()

        yield

        def finish(p):
            total = (mine[low(p), :, cols] + rf[l, :, cols]) * factor
            if k < n_out:
                out_o[:, k * TILE:(k + 1) * TILE] = total[:, :TILE]
            else:
                conv_o[:, c0:c0 + TILE] = total
            if size > TILE:
                bias_o[...] = total[:8, TILE:]

        @pl.when(place == 1)
        def _():
            both[0].wait_recv()
            mine[:, :, cols] += rz[l, :, :, cols]
            up.start()
            down.wait_recv()
            finish(1)

        yield

        @pl.when(place == 0)
        def _():
            up.wait_recv()
            finish(0)
            down.wait_send()

        pl.when(place == 1)(up.wait_send)
        pl.when(place == 2)(both[0].wait_send)
        pl.when(place == 3)(both[1].wait_send)
        yield

    chunks = [[chunk(l, k) for k in range(tiles)] for l in range(2)]

    def advance(l, *which):
        if fused:
            for k in which or range(tiles):
                next(chunks[l][k])

    def all_grads(l):
        if fused:
            return
        for k in range(tiles):
            grad_tile(l, k)
        bias_grad(l)

    every = pl.ds(0, rows)
    put_rows(0, B, 0, x[0, A, :])
    put_rows(0, B, chan, x[0, B, :])
    split_conv(0)
    forward(0, B)
    split_out(0)
    second_b = second_input(B)
    pl.when(has_next)(x2_copy[1].start)
    put_rows(0, A, chan, x[0, A, :])
    put_rows(1, B, chan, second_b)
    late, early = pl.ds(chan, chan), pl.ds(0, chan)
    turn_out(0)
    fetches["sk"].wait()
    skip = split(sk[0])
    dhs[0] = dot3(skip, (woth[0, late, :], wotl[0, late, :]), NN)
    pl.when(has_prev)(t_copy.wait_recv)
    put_rows(0, A, 0, tail[...])
    forward(0, A)
    second_a = second_input(A)
    pl.when(has_next)(x2_copy[0].start)
    put_rows(1, A, chan, second_a)
    split_conv(1)
    split_out(1)
    turn_out(1)
    fetches["c2"].wait()
    dhs[1] = dot3(skip, (woth[1, late, :], wotl[1, late, :]), NN) + dot3(
        split(c2[0]), (woth[1, early, :], wotl[1, early, :]), NN)
    turn_conv(1)
    for i in (1, 0):
        r = (A, B)[i]
        pl.when(has_prev)(x2_copy[i].wait_recv)
        put_rows(1, r, 0, x2p[r, :])
        forward(1, r)
        dmixed(1, r, dhs[1, r, :], i)
        q2[r, :] = back(1, r, 0)
        pl.when(has_prev)(q2_copy[i].start)
    for l in range(2):
        put_outer(l, every, chan, sk[0])
    put_outer(1, every, 0, c2[0])
    put_turned(1, every, 0, x2p[...])
    put_turned(1, every, chan, x2[...])
    all_grads(1)
    advance(1)
    c1[...] = c2[0] + back(1, every, chan)
    turn_conv(0)
    put_turned(0, B, 0, x[0, A, :])
    put_turned(0, A, 0, tail[...])
    put_turned(0, every, chan, x[0])
    advance(1)
    for i in (1, 0):
        r = (A, B)[i]
        pl.when(has_next)(q2_copy[i].wait_recv)
        carried = c1[r, :] + q2r[r, :]
        c1[r, :] = carried
        dmixed(0, r, dhs[0, r, :] + dot3(split(carried), (woth[0, early, :], wotl[0, early, :]), NN), i)
        q1[r, :] = back(0, r, 0)
        if i == 0:
            pl.when(has_prev)(q1_copy.start)
    put_outer(0, every, 0, c1[...])
    all_grads(0)
    for k in range(tiles):
        advance(0, k)
        advance(1, k)
    advance(0)
    advance(1)
    c1[...] = c1[...] + back(0, every, chan)
    ig[0, A, :] = c1[A, :] + q1[B, :]
    pl.when(has_next)(q1_copy.wait_recv)
    ig[0, B, :] = c1[B, :] + q1r[...]
    for stage in range(3):
        for k in range(tiles):
            advance(0, k)
            advance(1, k)
    advance(0)
    advance(0)
    pl.when(has_next)(t_copy.wait_send)
    for i in range(2):
        pl.when(has_next)(x2_copy[i].wait_send)
        pl.when(has_prev)(q2_copy[i].wait_send)
    pl.when(has_prev)(q1_copy.wait_send)
    for copy in copies:
        copy.wait_send()


def hand_on(a, b, c, bias, a_out, b_out, c_out, bias_out):
    a_out[...], b_out[...], c_out[...] = a[...], b[...], c[...]
    bias_out[...] = bias[0, : bias_out.shape[0]]


def local(n_seq, n_dp, *args):
    inputs, _, _, convolution_weight, _, output_weight = args
    _, rows, chan = inputs.shape
    half = rows // 2
    gate = output_weight.shape[1]
    fused = (n_seq, n_dp) == (8, 4)
    factor = 1.0 / math.sqrt(rows * n_seq * n_dp)
    block = 2 * (2 * chan) // (n_seq * n_dp)
    width = 3 * gate + 128
    vmem, sds = pltpu.VMEM, jax.ShapeDtypeStruct
    if fused:
        grads = [sds((block, 2 * gate), F32), sds((block, gate), F32), sds((8, 128), F32)]
    else:
        grads = [sds((2, 2 * chan, 2 * gate), F32), sds((2, 2 * chan, gate), F32), sds((2, 2 * gate), F32)]
    pair = lambda *shape: [vmem(shape, BF16)] * 2
    scratch = [
        *pair(2, 2 * chan, 2 * gate), *pair(2, gate, 2 * chan),
        *pair(2, 2 * gate, 2 * chan), *pair(2, 2 * chan, gate),
        *pair(2, rows, 2 * chan), *pair(2, 2 * chan, rows), *pair(2, rows, gate),
        vmem((2, rows, gate), F32), vmem((2, rows, gate), F32),
        *pair(2, 2 * chan, rows), vmem((2, rows, gate), F32), *pair(2, rows, 2 * gate),
        vmem((rows, chan), F32), vmem((rows, chan), F32), vmem((half, chan), F32),
        vmem((rows, chan), F32), vmem((rows, chan), F32), vmem((rows, chan), F32),
        vmem((half, chan), F32), vmem((rows, chan), F32), vmem((2, 8, 2 * gate), F32),
        vmem(inputs.shape, F32), vmem(inputs.shape, F32),
        vmem(convolution_weight.shape, F32), vmem(output_weight.shape, F32),
        pltpu.SemaphoreType.DMA((6 + 36 * gate // TILE,)), pltpu.SemaphoreType.DMA((6 + 36 * gate // TILE,)),
        pltpu.SemaphoreType.DMA((6,)),
    ]
    if fused:
        scratch += [
            vmem((2, 2, 2, 2, 2, block, width), F32), vmem((2, 2, 2, 2, block, width), F32),
            vmem((2, 2, 2, block, width), F32), vmem((2, 2, block, width), F32),
            vmem((2, 2, block, width), F32), vmem((2, block, width), F32),
        ]
    spec, anywhere = pl.BlockSpec(memory_space=pltpu.VMEM), pl.BlockSpec(memory_space=pl.ANY)
    input_grad, conv, out, bias = pl.pallas_call(
        functools.partial(kernel, n_seq, n_dp, fused, factor),
        out_shape=[sds(inputs.shape, F32)] + grads,
        in_specs=[spec, anywhere, anywhere, anywhere, spec, anywhere],
        out_specs=[spec] * 4,
        scratch_shapes=scratch,
        compiler_params=pltpu.CompilerParams(
            collective_id=0, has_side_effects=True, vmem_limit_bytes=60 * 1024 * 1024),
    )(*args)
    if fused:
        piece = 4 * gate // (n_seq * n_dp)
        return pl.pallas_call(
            hand_on,
            out_shape=[sds(inputs.shape, F32), *grads[:2], sds((piece,), F32)],
            in_specs=[spec] * 4,
            out_specs=[spec] * 4,
        )(input_grad, conv, out, bias)

    def scattered(terms):
        terms = terms.reshape((-1,) + terms.shape[2:]) * factor
        part = lax.psum_scatter(terms, "seq", scatter_dimension=0, tiled=True)
        return lax.psum_scatter(part, "dp", scatter_dimension=0, tiled=True)

    return input_grad, scattered(conv), scattered(out), scattered(bias)


def solution(mesh):
    return jax.shard_map(
        functools.partial(local, mesh.shape["seq"], mesh.shape["dp"]),
        mesh=mesh,
        in_specs=(P("dp", "seq", None),) * 3 + (P(), P(), P()),
        out_specs=(P("dp", "seq", None), P(("seq", "dp"), None), P(("seq", "dp"), None), P(("seq", "dp"))),
        check_vma=False,
    )
```

```python
import functools
import math

import jax
import jax.numpy as jnp
from jax import lax
from jax.experimental import pallas as pl
from jax.experimental.pallas import tpu as pltpu
from jax.sharding import PartitionSpec as P

F32, BF16 = jnp.float32, jnp.bfloat16
NN = (((1,), (0,)), ((), ()))
TILE = 256


def split(value):
    high = value.astype(BF16)
    return high, (value - high.astype(F32)).astype(BF16)


def dot3(left, right, dims):
    product = functools.partial(lax.dot_general, dimension_numbers=dims, preferred_element_type=F32)
    (lh, ll), (rh, rl) = left, right
    return (product(ll, rh) + product(lh, rl)) + product(lh, rh)


def kernel(n_seq, n_dp, fused, factor, *refs):
    refs = list(refs)
    x, c2_in, sk_in, cw_in, cb, ow_in = refs[:6]
    ig, conv_o, out_o, bias_o = refs[6:10]
    (wch, wcl, woh, wol, wcth, wctl, woth, wotl, jh, jl, jth, jtl, hh, hl, fa, ga, oth, otl, dhs, dzh, dzl,
     x2, x2p, tail, q2, q2r, q1, q1r, c1, bsum, c2, sk, cw, ow, ssem, rsem, lsem) = refs[10:47]
    if fused:
        grad, rc, r1, r2, rz, rf = refs[47:]
    rows, chan = x.shape[1], x.shape[2]
    half = rows // 2
    gate = ow_in.shape[1]
    width = 3 * gate + 128
    A, B = pl.ds(0, half), pl.ds(half, half)

    seq, dp = lax.axis_index("seq"), lax.axis_index("dp")
    has_next, has_prev = seq < n_seq - 1, seq > 0
    nxt, prv = lax.rem(seq + 1, n_seq), lax.rem(seq + n_seq - 1, n_seq)
    me_z, me_y, me_x, me_c = seq // 2, seq % 2, dp // 2, dp % 2

    fetches = {}
    for i, (name, src, dst) in enumerate((
        ("cw0", cw_in.at[0], cw.at[0]), ("ow0", ow_in.at[0], ow.at[0]), ("sk", sk_in, sk),
        ("c2", c2_in, c2), ("ow1", ow_in.at[1], ow.at[1]), ("cw1", cw_in.at[1], cw.at[1]))):
        fetches[name] = pltpu.make_async_copy(src, dst, lsem.at[i])
        fetches[name].start()

    barrier = pltpu.get_barrier_semaphore()
    greet = [(nxt, dp), (prv, dp)]
    if fused:
        greet += [(seq, 2 * me_x + 1 - me_c), (seq, 2 * (1 - me_x) + me_c), (2 * me_z + 1 - me_y, dp)]
        greet += [(lax.rem(seq + 2 * k, n_seq), dp) for k in range(1, n_seq // 2)]
    for s, d in greet:
        pl.semaphore_signal(barrier, inc=1, device_id=(s, d), device_id_type=pl.DeviceIdType.MESH)
    pl.semaphore_wait(barrier, len(greet))

    def remote(src, dst, send, recv, s, d):
        return pltpu.make_async_remote_copy(
            src_ref=src, dst_ref=dst, send_sem=ssem.at[send], recv_sem=rsem.at[recv],
            device_id=(s, d), device_id_type=pl.DeviceIdType.MESH)

    t_copy = remote(x.at[0, B], tail, 0, 0, nxt, dp)
    x2_copy = [remote(x2.at[r], x2p.at[r], 1 + i, 1 + i, nxt, dp) for i, r in enumerate((A, B))]
    q2_copy = [remote(q2.at[r], q2r.at[r], 3 + i, 3 + i, prv, dp) for i, r in enumerate((A, B))]
    q1_copy = remote(q1.at[A], q1r, 5, 5, prv, dp)

    pl.when(has_next)(t_copy.start)

    @pl.when(jnp.logical_not(has_prev))
    def _():
        tail[...] = jnp.zeros_like(tail)
        x2p[...] = jnp.zeros_like(x2p)

    @pl.when(jnp.logical_not(has_next))
    def _():
        q2r[...] = jnp.zeros_like(q2r)
        q1r[...] = jnp.zeros_like(q1r)

    def split_conv(l):
        fetches["cw%d" % l].wait()
        wch[l], wcl[l] = split(cw[l])

    def split_out(l):
        fetches["ow%d" % l].wait()
        woh[l], wol[l] = split(ow[l])

    def turn_conv(l):
        wcth[l], wctl[l] = split(cw[l].T)

    def turn_out(l):
        woth[l], wotl[l] = split(ow[l].T)

    def put_rows(l, r, c0, value):
        cols = pl.ds(c0, chan)
        jh[l, r, cols], jl[l, r, cols] = split(value)

    def put_turned(l, r, c0, value):
        cols = pl.ds(c0, chan)
        jth[l, cols, r], jtl[l, cols, r] = split(value.T)

    def put_outer(l, r, c0, value):
        cols = pl.ds(c0, chan)
        oth[l, cols, r], otl[l, cols, r] = split(value.T)

    def forward(l, r):
        joined = (jh[l, r, :], jl[l, r, :])
        for n in range(gate // TILE):
            cols, gcols = pl.ds(n * TILE, TILE), pl.ds(gate + n * TILE, TILE)
            f = dot3(joined, (wch[l, :, cols], wcl[l, :, cols]), NN) + cb[l:l + 1, cols]
            g = dot3(joined, (wch[l, :, gcols], wcl[l, :, gcols]), NN) + cb[l:l + 1, gcols]
            t, s = jnp.tanh(f), jax.nn.sigmoid(g)
            h = t * s
            fa[l, r, cols] = s * (1.0 - t * t)
            ga[l, r, cols] = h * (1.0 - s)
            hh[l, r, cols], hl[l, r, cols] = split(h)

    def second_input(r):
        out = pl.ds(0, chan)
        value = x[0, r, :] + dot3((hh[0, r, :], hl[0, r, :]), (woh[0, :, out], wol[0, :, out]), NN)
        x2[r, :] = value
        return value

    def dmixed(l, r, dh, i):
        df, dg = dh * fa[l, r, :], dh * ga[l, r, :]
        dzh[l, r, :gate], dzl[l, r, :gate] = split(df)
        dzh[l, r, gate:], dzl[l, r, gate:] = split(dg)
        bsum[l, i:i + 1, :gate] = jnp.sum(df, axis=0, keepdims=True)
        bsum[l, i:i + 1, gate:] = jnp.sum(dg, axis=0, keepdims=True)

    def back(l, r, c0):
        taps = pl.ds(c0, chan)
        return dot3((dzh[l, r, :], dzl[l, r, :]), (wcth[l, :, taps], wctl[l, :, taps]), NN)

    def put_grad(l, kind, c0, value):
        if not fused:
            (conv_o if kind == 0 else out_o)[l, :, c0:c0 + TILE] = value
            return
        c0 += kind * 2 * gate
        block = value.shape[0] // 16
        for j in range(16):
            grad[l, j % 2, j // 2 % 2, j // 4 % 2, j // 8, :, c0:c0 + TILE] = value[j * block:(j + 1) * block]

    def grad_tile(l, k):
        if k < n_out:
            cols = pl.ds(k * TILE, TILE)
            put_grad(l, 1, k * TILE, dot3((oth[l], otl[l]), (hh[l, :, cols], hl[l, :, cols]), NN))
            return
        c0 = (k - n_out) * TILE
        cols = pl.ds(c0, TILE)
        put_grad(l, 0, c0, dot3((jth[l], jtl[l]), (dzh[l, :, cols], dzl[l, :, cols]), NN))

    def bias_grad(l):
        total = bsum[l, 0:1, :] + bsum[l, 1:2, :]
        if not fused:
            bias_o[l:l + 1, :] = total
            return
        piece = 2 * gate // 16
        for j in range(16):
            spot = (l, j % 2, j // 2 % 2, j // 4 % 2, j // 8)
            grad[spot + (slice(None), slice(3 * gate, width))] = jnp.zeros((grad.shape[5], 128), F32)
            grad[spot + (slice(0, 1), slice(3 * gate, 3 * gate + piece))] = total[:, j * piece:(j + 1) * piece]

    n_out, tiles = gate // TILE, 3 * gate // TILE
    copies = []

    def go(src, dst, k, peer):
        copy = remote(src, dst, k, k, *peer)
        copy.start()
        copies.append(copy)
        return copy

    def chunk(l, k):
        base = 6 + 6 * (tiles * l + k)
        if k < n_out:
            c0, size = 2 * gate + k * TILE, TILE
        else:
            c0, size = (k - n_out) * TILE, TILE
        if k == n_out - 1:
            size += 128
        cols = pl.ds(c0, size)
        x_first = l == 1 or k % 2 == 1
        other_c = (seq, 2 * me_x + 1 - me_c)
        other_x = (seq, 2 * (1 - me_x) + me_c)
        other_y = (2 * me_z + 1 - me_y, dp)
        own = grad.at[l, me_c]
        place = me_z if l == 0 else 3 - me_z
        low = lambda p: p if l == 0 else 1 - p
        at_place = lambda p: (2 * (p if l == 0 else 3 - p) + me_y, dp)

        if k == n_out - 1:
            bias_grad(l)
        grad_tile(l, k)
        core = go(grad.at[l, 1 - me_c, :, :, :, :, cols], rc.at[l, :, :, :, :, cols], base, other_c)
        yield
        core.wait_recv()
        own[:, :, :, :, cols] += rc[l, :, :, :, :, cols]
        if x_first:
            first = go(own.at[1 - me_x, :, :, :, cols], r1.at[l, :, :, :, cols], base + 1, other_x)
        else:
            first = go(own.at[:, 1 - me_y, :, :, cols], r1.at[l, :, :, :, cols], base + 1, other_y)
        yield
        first.wait_recv()
        if x_first:
            own[me_x, :, :, :, cols] += r1[l, :, :, :, cols]
            second = go(own.at[me_x, 1 - me_y, :, :, cols], r2.at[l, :, :, cols], base + 2, other_y)
        else:
            own[:, me_y, :, :, cols] += r1[l, :, :, :, cols]
            second = go(own.at[1 - me_x, me_y, :, :, cols], r2.at[l, :, :, cols], base + 2, other_x)
        yield
        second.wait_recv()
        mine = own.at[me_x, me_y]
        mine[:, :, cols] += r2[l, :, :, cols]
        both = [remote(mine.at[:, :, cols], rz.at[l, :, :, cols], base + 3, base + 3, *at_place(p)) for p in (1, 2)]
        up = remote(mine.at[low(0), :, cols], rf.at[l, :, cols], base + 3, base + 4, *at_place(0))
        down = remote(mine.at[low(1), :, cols], rf.at[l, :, cols], base + 3, base + 4, *at_place(1))
        pl.when(place == 3)(both[1].start)
        pl.when(place == 0)(down.start)
        yield

        @pl.when(place == 2)
        def _():
            both[1].wait_recv()
            mine[:, :, cols] += rz[l, :, :, cols]
            both[0].start()

        yield

        def finish(p):
            total = (mine[low(p), :, cols] + rf[l, :, cols]) * factor
            if k < n_out:
                out_o[:, k * TILE:(k + 1) * TILE] = total[:, :TILE]
            else:
                conv_o[:, c0:c0 + TILE] = total
            if size > TILE:
                bias_o[...] = total[:8, TILE:]

        @pl.when(place == 1)
        def _():
            both[0].wait_recv()
            mine[:, :, cols] += rz[l, :, :, cols]
            up.start()
            down.wait_recv()
            finish(1)

        yield

        @pl.when(place == 0)
        def _():
            up.wait_recv()
            finish(0)
            down.wait_send()

        pl.when(place == 1)(up.wait_send)
        pl.when(place == 2)(both[0].wait_send)
        pl.when(place == 3)(both[1].wait_send)
        yield

    chunks = [[chunk(l, k) for k in range(tiles)] for l in range(2)]

    def advance(l, *which):
        if fused:
            for k in which or range(tiles):
                next(chunks[l][k])

    def all_grads(l):
        if fused:
            return
        for k in range(tiles):
            grad_tile(l, k)
        bias_grad(l)

    every = pl.ds(0, rows)
    put_rows(0, B, 0, x[0, A, :])
    put_rows(0, B, chan, x[0, B, :])
    split_conv(0)
    forward(0, B)
    split_out(0)
    second_b = second_input(B)
    pl.when(has_next)(x2_copy[1].start)
    put_rows(0, A, chan, x[0, A, :])
    put_rows(1, B, chan, second_b)
    late, early = pl.ds(chan, chan), pl.ds(0, chan)
    turn_out(0)
    fetches["sk"].wait()
    skip = split(sk[0])
    dhs[0] = dot3(skip, (woth[0, late, :], wotl[0, late, :]), NN)
    pl.when(has_prev)(t_copy.wait_recv)
    put_rows(0, A, 0, tail[...])
    forward(0, A)
    second_a = second_input(A)
    pl.when(has_next)(x2_copy[0].start)
    put_rows(1, A, chan, second_a)
    split_conv(1)
    split_out(1)
    turn_out(1)
    fetches["c2"].wait()
    dhs[1] = dot3(skip, (woth[1, late, :], wotl[1, late, :]), NN) + dot3(
        split(c2[0]), (woth[1, early, :], wotl[1, early, :]), NN)
    turn_conv(1)
    for i in (1, 0):
        r = (A, B)[i]
        pl.when(has_prev)(x2_copy[i].wait_recv)
        put_rows(1, r, 0, x2p[r, :])
        forward(1, r)
        dmixed(1, r, dhs[1, r, :], i)
        q2[r, :] = back(1, r, 0)
        pl.when(has_prev)(q2_copy[i].start)
    for l in range(2):
        put_outer(l, every, chan, sk[0])
    put_outer(1, every, 0, c2[0])
    put_turned(1, every, 0, x2p[...])
    put_turned(1, every, chan, x2[...])
    all_grads(1)
    advance(1)
    c1[...] = c2[0] + back(1, every, chan)
    turn_conv(0)
    put_turned(0, B, 0, x[0, A, :])
    put_turned(0, A, 0, tail[...])
    put_turned(0, every, chan, x[0])
    advance(1)
    for i in (1, 0):
        r = (A, B)[i]
        pl.when(has_next)(q2_copy[i].wait_recv)
        carried = c1[r, :] + q2r[r, :]
        c1[r, :] = carried
        dmixed(0, r, dhs[0, r, :] + dot3(split(carried), (woth[0, early, :], wotl[0, early, :]), NN), i)
        q1[r, :] = back(0, r, 0)
        if i == 0:
            pl.when(has_prev)(q1_copy.start)
    put_outer(0, every, 0, c1[...])
    all_grads(0)
    for k in range(tiles):
        advance(0, k)
        advance(1, k)
        if k > 1:
            advance(0, k - 2)
    advance(0, tiles - 2, tiles - 1)
    c1[...] = c1[...] + back(0, every, chan)
    ig[0, A, :] = c1[A, :] + q1[B, :]
    pl.when(has_next)(q1_copy.wait_recv)
    ig[0, B, :] = c1[B, :] + q1r[...]
    for tick in range(tiles + 6):
        for l, starts in ((1, (0, 1, 2, 3)), (0, (0, 2, 3, 4, 5))):
            for start in reversed(starts):
                if 0 <= tick - start < tiles:
                    advance(l, tick - start)
    pl.when(has_next)(t_copy.wait_send)
    for i in range(2):
        pl.when(has_next)(x2_copy[i].wait_send)
        pl.when(has_prev)(q2_copy[i].wait_send)
    pl.when(has_prev)(q1_copy.wait_send)
    for copy in copies:
        copy.wait_send()


def hand_on(a, b, c, bias, a_out, b_out, c_out, bias_out):
    a_out[...], b_out[...], c_out[...] = a[...], b[...], c[...]
    bias_out[...] = bias[0, : bias_out.shape[0]]


def local(n_seq, n_dp, *args):
    inputs, _, _, convolution_weight, _, output_weight = args
    _, rows, chan = inputs.shape
    half = rows // 2
    gate = output_weight.shape[1]
    fused = (n_seq, n_dp) == (8, 4)
    factor = 1.0 / math.sqrt(rows * n_seq * n_dp)
    block = 2 * (2 * chan) // (n_seq * n_dp)
    width = 3 * gate + 128
    vmem, sds = pltpu.VMEM, jax.ShapeDtypeStruct
    if fused:
        grads = [sds((block, 2 * gate), F32), sds((block, gate), F32), sds((8, 128), F32)]
    else:
        grads = [sds((2, 2 * chan, 2 * gate), F32), sds((2, 2 * chan, gate), F32), sds((2, 2 * gate), F32)]
    pair = lambda *shape: [vmem(shape, BF16)] * 2
    scratch = [
        *pair(2, 2 * chan, 2 * gate), *pair(2, gate, 2 * chan),
        *pair(2, 2 * gate, 2 * chan), *pair(2, 2 * chan, gate),
        *pair(2, rows, 2 * chan), *pair(2, 2 * chan, rows), *pair(2, rows, gate),
        vmem((2, rows, gate), F32), vmem((2, rows, gate), F32),
        *pair(2, 2 * chan, rows), vmem((2, rows, gate), F32), *pair(2, rows, 2 * gate),
        vmem((rows, chan), F32), vmem((rows, chan), F32), vmem((half, chan), F32),
        vmem((rows, chan), F32), vmem((rows, chan), F32), vmem((rows, chan), F32),
        vmem((half, chan), F32), vmem((rows, chan), F32), vmem((2, 8, 2 * gate), F32),
        vmem(inputs.shape, F32), vmem(inputs.shape, F32),
        vmem(convolution_weight.shape, F32), vmem(output_weight.shape, F32),
        pltpu.SemaphoreType.DMA((6 + 36 * gate // TILE,)), pltpu.SemaphoreType.DMA((6 + 36 * gate // TILE,)),
        pltpu.SemaphoreType.DMA((6,)),
    ]
    if fused:
        scratch += [
            vmem((2, 2, 2, 2, 2, block, width), F32), vmem((2, 2, 2, 2, block, width), F32),
            vmem((2, 2, 2, block, width), F32), vmem((2, 2, block, width), F32),
            vmem((2, 2, block, width), F32), vmem((2, block, width), F32),
        ]
    spec, anywhere = pl.BlockSpec(memory_space=pltpu.VMEM), pl.BlockSpec(memory_space=pl.ANY)
    input_grad, conv, out, bias = pl.pallas_call(
        functools.partial(kernel, n_seq, n_dp, fused, factor),
        out_shape=[sds(inputs.shape, F32)] + grads,
        in_specs=[spec, anywhere, anywhere, anywhere, spec, anywhere],
        out_specs=[spec] * 4,
        scratch_shapes=scratch,
        compiler_params=pltpu.CompilerParams(
            collective_id=0, has_side_effects=True, vmem_limit_bytes=60 * 1024 * 1024),
    )(*args)
    if fused:
        piece = 4 * gate // (n_seq * n_dp)
        return pl.pallas_call(
            hand_on,
            out_shape=[sds(inputs.shape, F32), *grads[:2], sds((piece,), F32)],
            in_specs=[spec] * 4,
            out_specs=[spec] * 4,
        )(input_grad, conv, out, bias)

    def scattered(terms):
        terms = terms.reshape((-1,) + terms.shape[2:]) * factor
        part = lax.psum_scatter(terms, "seq", scatter_dimension=0, tiled=True)
        return lax.psum_scatter(part, "dp", scatter_dimension=0, tiled=True)

    return input_grad, scattered(conv), scattered(out), scattered(bias)


def solution(mesh):
    return jax.shard_map(
        functools.partial(local, mesh.shape["seq"], mesh.shape["dp"]),
        mesh=mesh,
        in_specs=(P("dp", "seq", None),) * 3 + (P(), P(), P()),
        out_specs=(P("dp", "seq", None), P(("seq", "dp"), None), P(("seq", "dp"), None), P(("seq", "dp"))),
        check_vma=False,
    )
```

```python
import functools
import math

import jax
import jax.numpy as jnp
from jax import lax
from jax.experimental import pallas as pl
from jax.experimental.pallas import tpu as pltpu
from jax.sharding import PartitionSpec as P

F32, BF16 = jnp.float32, jnp.bfloat16
NN = (((1,), (0,)), ((), ()))
TILE = 256


def split(value):
    high = value.astype(BF16)
    return high, (value - high.astype(F32)).astype(BF16)


def dot3(left, right, dims):
    product = functools.partial(lax.dot_general, dimension_numbers=dims, preferred_element_type=F32)
    (lh, ll), (rh, rl) = left, right
    return (product(ll, rh) + product(lh, rl)) + product(lh, rh)


def kernel(n_seq, n_dp, fused, factor, *refs):
    refs = list(refs)
    x, c2_in, sk_in, cw_in, cb, ow_in = refs[:6]
    ig, conv_o, out_o, bias_o = refs[6:10]
    (wch, wcl, woh, wol, wcth, wctl, woth, wotl, jh, jl, jth, jtl, hh, hl, fa, ga, oth, otl, dhs, dzh, dzl,
     x2, x2p, tail, q2, q2r, q1, q1r, c1, bsum, c2, sk, cw, ow, ssem, rsem, lsem) = refs[10:47]
    if fused:
        grad, rc, r1, r2, rz, rf = refs[47:53]
        bias_refs, sums = refs[53:59], refs[59]
    rows, chan = x.shape[1], x.shape[2]
    half = rows // 2
    gate = ow_in.shape[1]
    A, B = pl.ds(0, half), pl.ds(half, half)

    seq, dp = lax.axis_index("seq"), lax.axis_index("dp")
    has_next, has_prev = seq < n_seq - 1, seq > 0
    nxt, prv = lax.rem(seq + 1, n_seq), lax.rem(seq + n_seq - 1, n_seq)
    me_z, me_y, me_x, me_c = seq // 2, seq % 2, dp // 2, dp % 2

    fetches = {}
    for i, (name, src, dst) in enumerate((
        ("cw0", cw_in.at[0], cw.at[0]), ("ow0", ow_in.at[0], ow.at[0]), ("sk", sk_in, sk),
        ("c2", c2_in, c2), ("ow1", ow_in.at[1], ow.at[1]), ("cw1", cw_in.at[1], cw.at[1]))):
        fetches[name] = pltpu.make_async_copy(src, dst, lsem.at[i])
        fetches[name].start()

    barrier = pltpu.get_barrier_semaphore()
    greet = [(nxt, dp), (prv, dp)]
    if fused:
        greet += [(seq, 2 * me_x + 1 - me_c), (seq, 2 * (1 - me_x) + me_c), (2 * me_z + 1 - me_y, dp)]
        greet += [(lax.rem(seq + 2 * k, n_seq), dp) for k in range(1, n_seq // 2)]
    for s, d in greet:
        pl.semaphore_signal(barrier, inc=1, device_id=(s, d), device_id_type=pl.DeviceIdType.MESH)
    pl.semaphore_wait(barrier, len(greet))

    def remote(src, dst, send, recv, s, d):
        return pltpu.make_async_remote_copy(
            src_ref=src, dst_ref=dst, send_sem=ssem.at[send], recv_sem=rsem.at[recv],
            device_id=(s, d), device_id_type=pl.DeviceIdType.MESH)

    t_copy = remote(x.at[0, B], tail, 0, 0, nxt, dp)
    x2_copy = [remote(x2.at[r], x2p.at[r], 1 + i, 1 + i, nxt, dp) for i, r in enumerate((A, B))]
    q2_copy = [remote(q2.at[r], q2r.at[r], 3 + i, 3 + i, prv, dp) for i, r in enumerate((A, B))]
    q1_copy = remote(q1.at[A], q1r, 5, 5, prv, dp)

    pl.when(has_next)(t_copy.start)

    @pl.when(jnp.logical_not(has_prev))
    def _():
        tail[...] = jnp.zeros_like(tail)
        x2p[...] = jnp.zeros_like(x2p)

    @pl.when(jnp.logical_not(has_next))
    def _():
        q2r[...] = jnp.zeros_like(q2r)
        q1r[...] = jnp.zeros_like(q1r)

    def tiled(extent, body, size=TILE):
        @pl.loop(0, extent // size)
        def _(n):
            body(pl.ds(pl.multiple_of(n * size, size), size))

    def split_conv(l):
        fetches["cw%d" % l].wait()

        def body(r):
            wch[l, r, :], wcl[l, r, :] = split(cw[l, r, :])
        tiled(2 * chan, body, 64)

    def split_out(l):
        fetches["ow%d" % l].wait()

        def body(r):
            woh[l, r, :], wol[l, r, :] = split(ow[l, r, :])
        tiled(gate, body, 64)

    def turn_conv(l):
        def body(r):
            wcth[l, r, :], wctl[l, r, :] = split(cw[l, :, r].T)
        tiled(2 * gate, body)

    def turn_out(l):
        def body(r):
            woth[l, r, :], wotl[l, r, :] = split(ow[l, :, r].T)
        tiled(2 * chan, body)

    def put_rows(l, r, c0, value):
        cols = pl.ds(c0, chan)
        jh[l, r, cols], jl[l, r, cols] = split(value)

    def put_turned(l, r, c0, value):
        cols = pl.ds(c0, chan)
        jth[l, cols, r], jtl[l, cols, r] = split(value.T)

    def put_outer(l, r, c0, value):
        cols = pl.ds(c0, chan)
        oth[l, cols, r], otl[l, cols, r] = split(value.T)

    def forward(l, r):
        @pl.loop(0, gate // TILE)
        def _(n):
            joined = (jh[l, r, :], jl[l, r, :])
            cols = pl.ds(pl.multiple_of(n * TILE, TILE), TILE)
            gcols = pl.ds(pl.multiple_of(gate + n * TILE, TILE), TILE)
            f = dot3(joined, (wch[l, :, cols], wcl[l, :, cols]), NN) + cb[l:l + 1, cols]
            g = dot3(joined, (wch[l, :, gcols], wcl[l, :, gcols]), NN) + cb[l:l + 1, gcols]
            t, s = jnp.tanh(f), jax.nn.sigmoid(g)
            h = t * s
            fa[l, r, cols] = s * (1.0 - t * t)
            ga[l, r, cols] = h * (1.0 - s)
            hh[l, r, cols], hl[l, r, cols] = split(h)

    def second_input(r):
        out = pl.ds(0, chan)
        value = x[0, r, :] + dot3((hh[0, r, :], hl[0, r, :]), (woh[0, :, out], wol[0, :, out]), NN)
        x2[r, :] = value
        return value

    def dmixed(l, r):
        @pl.loop(0, gate // TILE)
        def _(n):
            cols = pl.ds(pl.multiple_of(n * TILE, TILE), TILE)
            gcols = pl.ds(pl.multiple_of(gate + n * TILE, TILE), TILE)
            dh = dhs[l, r, cols]
            for part, where in ((dh * fa[l, r, cols], cols), (dh * ga[l, r, cols], gcols)):
                dzh[l, r, where], dzl[l, r, where] = split(part)
                total = jnp.sum(part, axis=0, keepdims=True)
                bsum[l, 0:1, where] = bsum[l, 0:1, where] + total

    def back(l, r, c0):
        taps = pl.ds(c0, chan)
        return dot3((dzh[l, r, :], dzl[l, r, :]), (wcth[l, :, taps], wctl[l, :, taps]), NN)

    n_out, n_conv = gate // TILE, 2 * gate // TILE
    tiles = n_out + n_conv

    def put_grad(l, kind, n, value):
        if not fused:
            (conv_o if kind == 0 else out_o)[l, :, pl.ds(pl.multiple_of(n * TILE, TILE), TILE)] = value
            return
        block = value.shape[0] // 16
        for j in range(16):
            grad[l, kind * n_conv + n, j % 2, j // 2 % 2, j // 4 % 2, j // 8] = value[j * block:(j + 1) * block]

    def gradients(l):
        @pl.loop(0, n_out)
        def _(n):
            cols = pl.ds(pl.multiple_of(n * TILE, TILE), TILE)
            put_grad(l, 1, n, dot3((oth[l], otl[l]), (hh[l, :, cols], hl[l, :, cols]), NN))
            step(l, n_conv + n, 0, "core")

        @pl.loop(0, n_conv)
        def _(n):
            cols = pl.ds(pl.multiple_of(n * TILE, TILE), TILE)
            put_grad(l, 0, n, dot3((jth[l], jtl[l]), (dzh[l, :, cols], dzl[l, :, cols]), NN))
            step(l, n, 0, "core")

        total = bsum[l, 0:1, :]
        if not fused:
            bias_o[l:l + 1, :] = total
            return
        piece, terms = 2 * gate // 16, bias_refs[0]
        terms[l] = jnp.zeros(terms.shape[1:], F32)
        for j in range(16):
            terms[l, j % 2, j // 2 % 2, j // 4 % 2, j // 8, 0:1, 0:piece] = total[:, j * piece:(j + 1) * piece]
        step(l, None, 0, "core")

    def step(l, k, odd, what):
        if not fused:
            return
        if k is None:
            mine, got_c, got_1, got_2, got_z, got_f = (ref.at[l] for ref in bias_refs)
            base = 6 + 6 * (2 * tiles + l)
        else:
            mine, got_c, got_1, got_2, got_z, got_f = (ref.at[l, k] for ref in (grad, rc, r1, r2, rz, rf))
            base = 6 + 6 * (tiles * l + k)
        other_c = (seq, 2 * me_x + 1 - me_c)
        other_x = (seq, 2 * (1 - me_x) + me_c)
        other_y = (2 * me_z + 1 - me_y, dp)
        place = me_z if l == 0 else 3 - me_z
        low = lambda p: p if l == 0 else 1 - p
        at_place = lambda p: (2 * (p if l == 0 else 3 - p) + me_y, dp)
        own = mine.at[me_c]
        last = own.at[me_x, me_y]
        core = remote(mine.at[1 - me_c], got_c, base, base, *other_c)
        if odd:
            first = remote(own.at[:, 1 - me_y], got_1, base + 1, base + 1, *other_y)
            second = remote(own.at[1 - me_x, me_y], got_2, base + 2, base + 2, *other_x)
        else:
            first = remote(own.at[1 - me_x], got_1, base + 1, base + 1, *other_x)
            second = remote(own.at[me_x, 1 - me_y], got_2, base + 2, base + 2, *other_y)
        to_1, to_2 = (remote(last, got_z, base + 3, base + 3, *at_place(p)) for p in (1, 2))
        up = remote(last.at[low(0)], got_f, base + 3, base + 4, *at_place(0))
        down = remote(last.at[low(1)], got_f, base + 3, base + 4, *at_place(1))

        def finish(p):
            total = (last[low(p)] + got_f[...]) * factor
            if k is None:
                bias_o[...] = total
            else:
                sums[k] = total

        if what == "core":
            core.start()
        elif what == "first":
            core.wait_recv()
            own[...] += got_c[...]
            first.start()
        elif what == "second":
            first.wait_recv()
            if odd:
                own[:, me_y] += got_1[...]
            else:
                own[me_x] += got_1[...]
            second.start()
        elif what == "z":
            second.wait_recv()
            last[...] += got_2[...]
            pl.when(place == 3)(to_2.start)
            pl.when(place == 0)(down.start)
        elif what == "relay":
            @pl.when(place == 2)
            def _():
                to_2.wait_recv()
                last[...] += got_z[...]
                to_1.start()
        elif what == "owner":
            @pl.when(place == 1)
            def _():
                to_1.wait_recv()
                last[...] += got_z[...]
                up.start()
                down.wait_recv()
                finish(1)
        elif what == "end":
            @pl.when(place == 0)
            def _():
                up.wait_recv()
                finish(0)
                down.wait_send()

            pl.when(place == 1)(up.wait_send)
            pl.when(place == 2)(to_1.wait_send)
            pl.when(place == 3)(to_2.wait_send)
            core.wait_send()
            first.wait_send()
            second.wait_send()

    def advance(*moves):
        if not fused:
            return
        longest = max(behind for _, _, behind in moves)

        @pl.loop(0, tiles // 2 + longest)
        def _(tick):
            for l, what, behind in moves:
                def body(l=l, what=what, behind=behind):
                    for odd in range(2):
                        step(l, 2 * (tick - behind) + odd, odd, what)
                if longest == 0:
                    body()
                else:
                    pl.when(jnp.logical_and(tick >= behind, tick < behind + tiles // 2))(body)

        for l, what, _ in moves:
            step(l, None, 0, what)

    bsum[...] = jnp.zeros_like(bsum)
    every = pl.ds(0, rows)
    put_rows(0, B, 0, x[0, A, :])
    put_rows(0, B, chan, x[0, B, :])
    split_conv(0)
    forward(0, B)
    split_out(0)
    second_b = second_input(B)
    pl.when(has_next)(x2_copy[1].start)
    put_rows(0, A, chan, x[0, A, :])
    put_rows(1, B, chan, second_b)
    late, early = pl.ds(chan, chan), pl.ds(0, chan)
    turn_out(0)
    fetches["sk"].wait()
    skip = split(sk[0])
    dhs[0] = dot3(skip, (woth[0, late, :], wotl[0, late, :]), NN)
    pl.when(has_prev)(t_copy.wait_recv)
    put_rows(0, A, 0, tail[...])
    forward(0, A)
    second_a = second_input(A)
    pl.when(has_next)(x2_copy[0].start)
    put_rows(1, A, chan, second_a)
    split_conv(1)
    split_out(1)
    turn_out(1)
    fetches["c2"].wait()
    dhs[1] = dot3(skip, (woth[1, late, :], wotl[1, late, :]), NN) + dot3(
        split(c2[0]), (woth[1, early, :], wotl[1, early, :]), NN)
    turn_conv(1)
    def half_copy(src, dst, base, i, peer):
        r = pl.ds(pl.multiple_of(i * half, half), half)
        return r, remote(src.at[r], dst.at[r], base + i, base + i, peer, dp)

    @pl.loop(0, 2)
    def _(n):
        r, landed = half_copy(x2, x2p, 1, 1 - n, nxt)
        pl.when(has_prev)(landed.wait_recv)
        put_rows(1, r, 0, x2p[r, :])
        forward(1, r)
        dmixed(1, r)
        q2[r, :] = back(1, r, 0)
        _, leaving = half_copy(q2, q2r, 3, 1 - n, prv)
        pl.when(has_prev)(leaving.start)

    @pl.loop(0, 2)
    def _(n):
        r = pl.ds(pl.multiple_of(n * half, half), half)
        for l in range(2):
            put_outer(l, r, chan, sk[0, r, :])
        put_outer(1, r, 0, c2[0, r, :])
        put_turned(1, r, 0, x2p[r, :])
        put_turned(1, r, chan, x2[r, :])

    gradients(1)

    @pl.loop(0, 2)
    def _(n):
        r = pl.ds(pl.multiple_of(n * half, half), half)
        c1[r, :] = c2[0, r, :] + back(1, r, chan)
        put_turned(0, r, chan, x[0, r, :])

    turn_conv(0)
    put_turned(0, B, 0, x[0, A, :])
    put_turned(0, A, 0, tail[...])
    advance((1, "first", 0))

    @pl.loop(0, 2)
    def _(n):
        r, landed = half_copy(q2, q2r, 3, 1 - n, prv)
        pl.when(has_next)(landed.wait_recv)
        carried = c1[r, :] + q2r[r, :]
        c1[r, :] = carried
        dhs[0, r, :] += dot3(split(carried), (woth[0, early, :], wotl[0, early, :]), NN)
        dmixed(0, r)
        q1[r, :] = back(0, r, 0)

    pl.when(has_prev)(q1_copy.start)

    @pl.loop(0, 2)
    def _(n):
        r = pl.ds(pl.multiple_of(n * half, half), half)
        put_outer(0, r, 0, c1[r, :])

    gradients(0)
    advance((0, "first", 0))
    advance((1, "second", 0))

    @pl.loop(0, 2)
    def _(n):
        r = pl.ds(pl.multiple_of(n * half, half), half)
        c1[r, :] += back(0, r, chan)

    ig[0, A, :] = c1[A, :] + q1[B, :]
    pl.when(has_next)(q1_copy.wait_recv)
    ig[0, B, :] = c1[B, :] + q1r[...]
    advance((1, "z", 0), (0, "second", 0), (1, "relay", 1), (0, "z", 1), (1, "owner", 2), (0, "relay", 2))
    advance((0, "owner", 0))
    advance((0, "end", 0))
    advance((1, "end", 0))
    if fused:
        for n in range(n_conv):
            conv_o[:, n * TILE:(n + 1) * TILE] = sums[n]
        for n in range(n_out):
            out_o[:, n * TILE:(n + 1) * TILE] = sums[n_conv + n]
    pl.when(has_next)(t_copy.wait_send)
    for i in range(2):
        pl.when(has_next)(x2_copy[i].wait_send)
        pl.when(has_prev)(q2_copy[i].wait_send)
    pl.when(has_prev)(q1_copy.wait_send)


def hand_on(a, b, c, bias, a_out, b_out, c_out, bias_out):
    a_out[...], b_out[...], c_out[...] = a[...], b[...], c[...]
    bias_out[...] = bias[0, : bias_out.shape[0]]


def local(n_seq, n_dp, *args):
    inputs, _, _, convolution_weight, _, output_weight = args
    _, rows, chan = inputs.shape
    half = rows // 2
    gate = output_weight.shape[1]
    fused = (n_seq, n_dp) == (8, 4)
    factor = 1.0 / math.sqrt(rows * n_seq * n_dp)
    block = 2 * (2 * chan) // (n_seq * n_dp)
    vmem, sds = pltpu.VMEM, jax.ShapeDtypeStruct
    if fused:
        grads = [sds((block, 2 * gate), F32), sds((block, gate), F32), sds((8, 128), F32)]
    else:
        grads = [sds((2, 2 * chan, 2 * gate), F32), sds((2, 2 * chan, gate), F32), sds((2, 2 * gate), F32)]
    pair = lambda *shape: [vmem(shape, BF16)] * 2
    scratch = [
        *pair(2, 2 * chan, 2 * gate), *pair(2, gate, 2 * chan),
        *pair(2, 2 * gate, 2 * chan), *pair(2, 2 * chan, gate),
        *pair(2, rows, 2 * chan), *pair(2, 2 * chan, rows), *pair(2, rows, gate),
        vmem((2, rows, gate), F32), vmem((2, rows, gate), F32),
        *pair(2, 2 * chan, rows), vmem((2, rows, gate), F32), *pair(2, rows, 2 * gate),
        vmem((rows, chan), F32), vmem((rows, chan), F32), vmem((half, chan), F32),
        vmem((rows, chan), F32), vmem((rows, chan), F32), vmem((rows, chan), F32),
        vmem((half, chan), F32), vmem((rows, chan), F32), vmem((2, 8, 2 * gate), F32),
        vmem(inputs.shape, F32), vmem(inputs.shape, F32),
        vmem(convolution_weight.shape, F32), vmem(output_weight.shape, F32),
        pltpu.SemaphoreType.DMA((18 + 36 * gate // TILE,)), pltpu.SemaphoreType.DMA((18 + 36 * gate // TILE,)),
        pltpu.SemaphoreType.DMA((6,)),
    ]
    if fused:
        tiles = 3 * gate // 256
        for lead, tile in (((2, tiles), (block, 256)), ((2,), (8, 128))):
            for between in ((2, 2, 2, 2), (2, 2, 2), (2, 2), (2,), (2,), ()):
                scratch.append(vmem(lead + between + tile, F32))
        scratch.append(vmem((tiles, block, 256), F32))
    spec, anywhere = pl.BlockSpec(memory_space=pltpu.VMEM), pl.BlockSpec(memory_space=pl.ANY)
    input_grad, conv, out, bias = pl.pallas_call(
        functools.partial(kernel, n_seq, n_dp, fused, factor),
        out_shape=[sds(inputs.shape, F32)] + grads,
        in_specs=[spec, anywhere, anywhere, anywhere, spec, anywhere],
        out_specs=[spec] * 4,
        scratch_shapes=scratch,
        compiler_params=pltpu.CompilerParams(
            collective_id=0, has_side_effects=True, vmem_limit_bytes=60 * 1024 * 1024),
    )(*args)
    if fused:
        piece = 4 * gate // (n_seq * n_dp)
        return pl.pallas_call(
            hand_on,
            out_shape=[sds(inputs.shape, F32), *grads[:2], sds((piece,), F32)],
            in_specs=[spec] * 4,
            out_specs=[spec] * 4,
        )(input_grad, conv, out, bias)

    def scattered(terms):
        terms = terms.reshape((-1,) + terms.shape[2:]) * factor
        part = lax.psum_scatter(terms, "seq", scatter_dimension=0, tiled=True)
        return lax.psum_scatter(part, "dp", scatter_dimension=0, tiled=True)

    return input_grad, scattered(conv), scattered(out), scattered(bias)


def solution(mesh):
    return jax.shard_map(
        functools.partial(local, mesh.shape["seq"], mesh.shape["dp"]),
        mesh=mesh,
        in_specs=(P("dp", "seq", None),) * 3 + (P(), P(), P()),
        out_specs=(P("dp", "seq", None), P(("seq", "dp"), None), P(("seq", "dp"), None), P(("seq", "dp"))),
        check_vma=False,
    )
```

```python
import functools
import math

import jax
import jax.numpy as jnp
from jax import lax
from jax.experimental import pallas as pl
from jax.experimental.pallas import tpu as pltpu
from jax.sharding import PartitionSpec as P

F32, BF16 = jnp.float32, jnp.bfloat16
NN = (((1,), (0,)), ((), ()))
TILE = 256


def unrolled(start, stop):
    return lambda body: [body(n) for n in range(start, stop)]


def split(value):
    high = value.astype(BF16)
    return high, (value - high.astype(F32)).astype(BF16)


def dot3(left, right, dims):
    product = functools.partial(lax.dot_general, dimension_numbers=dims, preferred_element_type=F32)
    (lh, ll), (rh, rl) = left, right
    return (product(ll, rh) + product(lh, rl)) + product(lh, rh)


def kernel(n_seq, n_dp, fused, factor, *refs):
    refs = list(refs)
    x, c2_in, sk_in, cw_in, cb, ow_in = refs[:6]
    ig, conv_o, out_o, bias_o = refs[6:10]
    (wch, wcl, woh, wol, wcth, wctl, woth, wotl, jh, jl, jth, jtl, hh, hl, fa, ga, oth, otl, dhs, dzh, dzl,
     x2, x2p, tail, q2, q2r, q1, q1r, c1, bsum, c2, sk, cw, ow, ssem, rsem, lsem) = refs[10:47]
    if fused:
        grad, rc, r1, r2, rz, rf = refs[47:53]
        bias_refs, sums = refs[53:59], refs[59]
    rows, chan = x.shape[1], x.shape[2]
    half = rows // 2
    gate = ow_in.shape[1]
    A, B = pl.ds(0, half), pl.ds(half, half)

    seq, dp = lax.axis_index("seq"), lax.axis_index("dp")
    has_next, has_prev = seq < n_seq - 1, seq > 0
    nxt, prv = lax.rem(seq + 1, n_seq), lax.rem(seq + n_seq - 1, n_seq)
    me_z, me_y, me_x, me_c = seq // 2, seq % 2, dp // 2, dp % 2

    fetches = {}
    for i, (name, src, dst) in enumerate((
        ("cw0", cw_in.at[0], cw.at[0]), ("ow0", ow_in.at[0], ow.at[0]), ("sk", sk_in, sk),
        ("c2", c2_in, c2), ("ow1", ow_in.at[1], ow.at[1]), ("cw1", cw_in.at[1], cw.at[1]))):
        fetches[name] = pltpu.make_async_copy(src, dst, lsem.at[i])
        fetches[name].start()

    barrier = pltpu.get_barrier_semaphore()
    greet = [(nxt, dp), (prv, dp)]
    if fused:
        greet += [(seq, 2 * me_x + 1 - me_c), (seq, 2 * (1 - me_x) + me_c), (2 * me_z + 1 - me_y, dp)]
        greet += [(lax.rem(seq + 2 * k, n_seq), dp) for k in range(1, n_seq // 2)]
    for s, d in greet:
        pl.semaphore_signal(barrier, inc=1, device_id=(s, d), device_id_type=pl.DeviceIdType.MESH)
    pl.semaphore_wait(barrier, len(greet))

    def remote(src, dst, send, recv, s, d):
        return pltpu.make_async_remote_copy(
            src_ref=src, dst_ref=dst, send_sem=ssem.at[send], recv_sem=rsem.at[recv],
            device_id=(s, d), device_id_type=pl.DeviceIdType.MESH)

    t_copy = remote(x.at[0, B], tail, 0, 0, nxt, dp)
    x2_copy = [remote(x2.at[r], x2p.at[r], 1 + i, 1 + i, nxt, dp) for i, r in enumerate((A, B))]
    q2_copy = [remote(q2.at[r], q2r.at[r], 3 + i, 3 + i, prv, dp) for i, r in enumerate((A, B))]
    q1_copy = remote(q1.at[A], q1r, 5, 5, prv, dp)

    pl.when(has_next)(t_copy.start)

    @pl.when(jnp.logical_not(has_prev))
    def _():
        tail[...] = jnp.zeros_like(tail)
        x2p[...] = jnp.zeros_like(x2p)

    @pl.when(jnp.logical_not(has_next))
    def _():
        q2r[...] = jnp.zeros_like(q2r)
        q1r[...] = jnp.zeros_like(q1r)

    def tiled(extent, body, size=TILE):
        @unrolled(0, extent // size)
        def _(n):
            body(pl.ds(n * size, size))

    def split_conv(l):
        fetches["cw%d" % l].wait()

        def body(r):
            wch[l, r, :], wcl[l, r, :] = split(cw[l, r, :])
        tiled(2 * chan, body)

    def split_out(l):
        fetches["ow%d" % l].wait()

        def body(r):
            woh[l, r, :], wol[l, r, :] = split(ow[l, r, :])
        tiled(gate, body)

    def turn_conv(l):
        def body(r):
            wcth[l, r, :], wctl[l, r, :] = split(cw[l, :, r].T)
        tiled(2 * gate, body)

    def turn_out(l):
        def body(r):
            woth[l, r, :], wotl[l, r, :] = split(ow[l, :, r].T)
        tiled(2 * chan, body)

    def put_rows(l, r, c0, value):
        cols = pl.ds(c0, chan)
        jh[l, r, cols], jl[l, r, cols] = split(value)

    def put_turned(l, r, c0, value):
        cols = pl.ds(c0, chan)
        jth[l, cols, r], jtl[l, cols, r] = split(value.T)

    def put_outer(l, r, c0, value):
        cols = pl.ds(c0, chan)
        oth[l, cols, r], otl[l, cols, r] = split(value.T)

    def forward(l, r):
        @unrolled(0, gate // TILE)
        def _(n):
            joined = (jh[l, r, :], jl[l, r, :])
            cols = pl.ds(n * TILE, TILE)
            gcols = pl.ds(gate + n * TILE, TILE)
            f = dot3(joined, (wch[l, :, cols], wcl[l, :, cols]), NN) + cb[l:l + 1, cols]
            g = dot3(joined, (wch[l, :, gcols], wcl[l, :, gcols]), NN) + cb[l:l + 1, gcols]
            t, s = jnp.tanh(f), jax.nn.sigmoid(g)
            h = t * s
            fa[l, r, cols] = s * (1.0 - t * t)
            ga[l, r, cols] = h * (1.0 - s)
            hh[l, r, cols], hl[l, r, cols] = split(h)

    def second_input(r):
        out = pl.ds(0, chan)
        value = x[0, r, :] + dot3((hh[0, r, :], hl[0, r, :]), (woh[0, :, out], wol[0, :, out]), NN)
        x2[r, :] = value
        return value

    def dmixed(l, r):
        @unrolled(0, gate // TILE)
        def _(n):
            cols = pl.ds(n * TILE, TILE)
            gcols = pl.ds(gate + n * TILE, TILE)
            dh = dhs[l, r, cols]
            for part, where in ((dh * fa[l, r, cols], cols), (dh * ga[l, r, cols], gcols)):
                dzh[l, r, where], dzl[l, r, where] = split(part)
                total = jnp.sum(part, axis=0, keepdims=True)
                bsum[l, 0:1, where] = bsum[l, 0:1, where] + total

    def back(l, r, c0):
        taps = pl.ds(c0, chan)
        return dot3((dzh[l, r, :], dzl[l, r, :]), (wcth[l, :, taps], wctl[l, :, taps]), NN)

    n_out, n_conv = gate // TILE, 2 * gate // TILE
    tiles = n_out + n_conv

    def put_grad(l, kind, n, value):
        if not fused:
            (conv_o if kind == 0 else out_o)[l, :, pl.ds(n * TILE, TILE)] = value
            return
        block = value.shape[0] // 16
        for j in range(16):
            grad[l, kind * n_conv + n, j % 2, j // 2 % 2, j // 4 % 2, j // 8] = value[j * block:(j + 1) * block]

    def gradients(l):
        @unrolled(0, n_out)
        def _(n):
            cols = pl.ds(n * TILE, TILE)
            put_grad(l, 1, n, dot3((oth[l], otl[l]), (hh[l, :, cols], hl[l, :, cols]), NN))
            step(l, n_conv + n, 0, "core")

        @unrolled(0, n_conv)
        def _(n):
            cols = pl.ds(n * TILE, TILE)
            put_grad(l, 0, n, dot3((jth[l], jtl[l]), (dzh[l, :, cols], dzl[l, :, cols]), NN))
            step(l, n, 0, "core")

        total = bsum[l, 0:1, :]
        if not fused:
            bias_o[l:l + 1, :] = total
            return
        piece, terms = 2 * gate // 16, bias_refs[0]
        terms[l] = jnp.zeros(terms.shape[1:], F32)
        for j in range(16):
            terms[l, j % 2, j // 2 % 2, j // 4 % 2, j // 8, 0:1, 0:piece] = total[:, j * piece:(j + 1) * piece]
        step(l, None, 0, "core")

    def step(l, k, odd, what):
        if not fused:
            return
        if k is None:
            mine, got_c, got_1, got_2, got_z, got_f = (ref.at[l] for ref in bias_refs)
            base = 6 + 6 * (2 * tiles + l)
        else:
            mine, got_c, got_1, got_2, got_z, got_f = (ref.at[l, k] for ref in (grad, rc, r1, r2, rz, rf))
            base = 6 + 6 * (tiles * l + k)
        other_c = (seq, 2 * me_x + 1 - me_c)
        other_x = (seq, 2 * (1 - me_x) + me_c)
        other_y = (2 * me_z + 1 - me_y, dp)
        place = me_z if l == 0 else 3 - me_z
        low = lambda p: p if l == 0 else 1 - p
        at_place = lambda p: (2 * (p if l == 0 else 3 - p) + me_y, dp)
        own = mine.at[me_c]
        last = own.at[me_x, me_y]
        core = remote(mine.at[1 - me_c], got_c, base, base, *other_c)
        if odd:
            first = remote(own.at[:, 1 - me_y], got_1, base + 1, base + 1, *other_y)
            second = remote(own.at[1 - me_x, me_y], got_2, base + 2, base + 2, *other_x)
        else:
            first = remote(own.at[1 - me_x], got_1, base + 1, base + 1, *other_x)
            second = remote(own.at[me_x, 1 - me_y], got_2, base + 2, base + 2, *other_y)
        to_1, to_2 = (remote(last, got_z, base + 3, base + 3, *at_place(p)) for p in (1, 2))
        up = remote(last.at[low(0)], got_f, base + 3, base + 4, *at_place(0))
        down = remote(last.at[low(1)], got_f, base + 3, base + 4, *at_place(1))

        def finish(p):
            total = (last[low(p)] + got_f[...]) * factor
            if k is None:
                bias_o[...] = total
            else:
                sums[k] = total

        if what == "core":
            core.start()
        elif what == "first":
            core.wait_recv()
            own[...] += got_c[...]
            first.start()
        elif what == "second":
            first.wait_recv()
            if odd:
                own[:, me_y] += got_1[...]
            else:
                own[me_x] += got_1[...]
            second.start()
        elif what == "z":
            second.wait_recv()
            last[...] += got_2[...]
            pl.when(place == 3)(to_2.start)
            pl.when(place == 0)(down.start)
        elif what == "relay":
            @pl.when(place == 2)
            def _():
                to_2.wait_recv()
                last[...] += got_z[...]
                to_1.start()
        elif what == "owner":
            @pl.when(place == 1)
            def _():
                to_1.wait_recv()
                last[...] += got_z[...]
                up.start()
                down.wait_recv()
                finish(1)
        elif what == "end":
            @pl.when(place == 0)
            def _():
                up.wait_recv()
                finish(0)
                down.wait_send()

            pl.when(place == 1)(up.wait_send)
            pl.when(place == 2)(to_1.wait_send)
            pl.when(place == 3)(to_2.wait_send)
            core.wait_send()
            first.wait_send()
            second.wait_send()

    def advance(l, what, which=range(tiles + 1)):
        for k in which:
            step(l, k if k < tiles else None, k % 2, what)

    bsum[...] = jnp.zeros_like(bsum)
    every = pl.ds(0, rows)
    put_rows(0, B, 0, x[0, A, :])
    put_rows(0, B, chan, x[0, B, :])
    split_conv(0)
    forward(0, B)
    split_out(0)
    second_b = second_input(B)
    pl.when(has_next)(x2_copy[1].start)
    put_rows(0, A, chan, x[0, A, :])
    put_rows(1, B, chan, second_b)
    late, early = pl.ds(chan, chan), pl.ds(0, chan)
    turn_out(0)
    fetches["sk"].wait()
    skip = split(sk[0])
    dhs[0] = dot3(skip, (woth[0, late, :], wotl[0, late, :]), NN)
    pl.when(has_prev)(t_copy.wait_recv)
    put_rows(0, A, 0, tail[...])
    forward(0, A)
    second_a = second_input(A)
    pl.when(has_next)(x2_copy[0].start)
    put_rows(1, A, chan, second_a)
    split_conv(1)
    split_out(1)
    turn_out(1)
    fetches["c2"].wait()
    dhs[1] = dot3(skip, (woth[1, late, :], wotl[1, late, :]), NN) + dot3(
        split(c2[0]), (woth[1, early, :], wotl[1, early, :]), NN)
    turn_conv(1)
    def half_copy(src, dst, base, i, peer):
        r = pl.ds(i * half, half)
        return r, remote(src.at[r], dst.at[r], base + i, base + i, peer, dp)

    @unrolled(0, 2)
    def _(n):
        r, landed = half_copy(x2, x2p, 1, 1 - n, nxt)
        pl.when(has_prev)(landed.wait_recv)
        put_rows(1, r, 0, x2p[r, :])
        forward(1, r)
        dmixed(1, r)
        q2[r, :] = back(1, r, 0)
        _, leaving = half_copy(q2, q2r, 3, 1 - n, prv)
        pl.when(has_prev)(leaving.start)

    @unrolled(0, 2)
    def _(n):
        r = pl.ds(n * half, half)
        for l in range(2):
            put_outer(l, r, chan, sk[0, r, :])
        put_outer(1, r, 0, c2[0, r, :])
        put_turned(1, r, 0, x2p[r, :])
        put_turned(1, r, chan, x2[r, :])

    gradients(1)

    @unrolled(0, 2)
    def _(n):
        r = pl.ds(n * half, half)
        c1[r, :] = c2[0, r, :] + back(1, r, chan)
        put_turned(0, r, chan, x[0, r, :])

    turn_conv(0)
    put_turned(0, B, 0, x[0, A, :])
    put_turned(0, A, 0, tail[...])
    x_first, y_first = range(0, tiles + 1, 2), range(1, tiles + 1, 2)
    advance(1, "first", x_first)

    @unrolled(0, 2)
    def _(n):
        r, landed = half_copy(q2, q2r, 3, 1 - n, prv)
        pl.when(has_next)(landed.wait_recv)
        carried = c1[r, :] + q2r[r, :]
        c1[r, :] = carried
        dhs[0, r, :] += dot3(split(carried), (woth[0, early, :], wotl[0, early, :]), NN)
        dmixed(0, r)
        q1[r, :] = back(0, r, 0)

    pl.when(has_prev)(q1_copy.start)
    advance(1, "first", y_first)

    @unrolled(0, 2)
    def _(n):
        r = pl.ds(n * half, half)
        put_outer(0, r, 0, c1[r, :])

    gradients(0)
    advance(0, "first")
    advance(1, "second", x_first)

    @unrolled(0, 2)
    def _(n):
        r = pl.ds(n * half, half)
        c1[r, :] += back(0, r, chan)

    ig[0, A, :] = c1[A, :] + q1[B, :]
    pl.when(has_next)(q1_copy.wait_recv)
    ig[0, B, :] = c1[B, :] + q1r[...]
    advance(1, "second", y_first)
    stages = [(1, "z", 0), (1, "relay", 1), (1, "owner", 2), (1, "end", 3)]
    stages += [(0, "second", 0), (0, "z", 2), (0, "relay", 3), (0, "owner", 4), (0, "end", 5)]
    for tick in range(tiles + 6):
        for l, what, behind in stages:
            if 0 <= tick - behind <= tiles:
                advance(l, what, (tick - behind,))
    if fused:
        for n in range(n_conv):
            conv_o[:, n * TILE:(n + 1) * TILE] = sums[n]
        for n in range(n_out):
            out_o[:, n * TILE:(n + 1) * TILE] = sums[n_conv + n]
    pl.when(has_next)(t_copy.wait_send)
    for i in range(2):
        pl.when(has_next)(x2_copy[i].wait_send)
        pl.when(has_prev)(q2_copy[i].wait_send)
    pl.when(has_prev)(q1_copy.wait_send)


def hand_on(a, b, c, bias, a_out, b_out, c_out, bias_out):
    a_out[...], b_out[...], c_out[...] = a[...], b[...], c[...]
    bias_out[...] = bias[0, : bias_out.shape[0]]


def local(n_seq, n_dp, *args):
    inputs, _, _, convolution_weight, _, output_weight = args
    _, rows, chan = inputs.shape
    half = rows // 2
    gate = output_weight.shape[1]
    fused = (n_seq, n_dp) == (8, 4)
    factor = 1.0 / math.sqrt(rows * n_seq * n_dp)
    block = 2 * (2 * chan) // (n_seq * n_dp)
    vmem, sds = pltpu.VMEM, jax.ShapeDtypeStruct
    if fused:
        grads = [sds((block, 2 * gate), F32), sds((block, gate), F32), sds((8, 128), F32)]
    else:
        grads = [sds((2, 2 * chan, 2 * gate), F32), sds((2, 2 * chan, gate), F32), sds((2, 2 * gate), F32)]
    pair = lambda *shape: [vmem(shape, BF16)] * 2
    scratch = [
        *pair(2, 2 * chan, 2 * gate), *pair(2, gate, 2 * chan),
        *pair(2, 2 * gate, 2 * chan), *pair(2, 2 * chan, gate),
        *pair(2, rows, 2 * chan), *pair(2, 2 * chan, rows), *pair(2, rows, gate),
        vmem((2, rows, gate), F32), vmem((2, rows, gate), F32),
        *pair(2, 2 * chan, rows), vmem((2, rows, gate), F32), *pair(2, rows, 2 * gate),
        vmem((rows, chan), F32), vmem((rows, chan), F32), vmem((half, chan), F32),
        vmem((rows, chan), F32), vmem((rows, chan), F32), vmem((rows, chan), F32),
        vmem((half, chan), F32), vmem((rows, chan), F32), vmem((2, 8, 2 * gate), F32),
        vmem(inputs.shape, F32), vmem(inputs.shape, F32),
        vmem(convolution_weight.shape, F32), vmem(output_weight.shape, F32),
        pltpu.SemaphoreType.DMA((18 + 36 * gate // TILE,)), pltpu.SemaphoreType.DMA((18 + 36 * gate // TILE,)),
        pltpu.SemaphoreType.DMA((6,)),
    ]
    if fused:
        tiles = 3 * gate // 256
        for lead, tile in (((2, tiles), (block, 256)), ((2,), (8, 128))):
            for between in ((2, 2, 2, 2), (2, 2, 2), (2, 2), (2,), (2,), ()):
                scratch.append(vmem(lead + between + tile, F32))
        scratch.append(vmem((tiles, block, 256), F32))
    spec, anywhere = pl.BlockSpec(memory_space=pltpu.VMEM), pl.BlockSpec(memory_space=pl.ANY)
    input_grad, conv, out, bias = pl.pallas_call(
        functools.partial(kernel, n_seq, n_dp, fused, factor),
        out_shape=[sds(inputs.shape, F32)] + grads,
        in_specs=[spec, anywhere, anywhere, anywhere, spec, anywhere],
        out_specs=[spec] * 4,
        scratch_shapes=scratch,
        compiler_params=pltpu.CompilerParams(
            collective_id=0, has_side_effects=True, vmem_limit_bytes=60 * 1024 * 1024),
    )(*args)
    if fused:
        piece = 4 * gate // (n_seq * n_dp)
        return pl.pallas_call(
            hand_on,
            out_shape=[sds(inputs.shape, F32), *grads[:2], sds((piece,), F32)],
            in_specs=[spec] * 4,
            out_specs=[spec] * 4,
        )(input_grad, conv, out, bias)

    def scattered(terms):
        terms = terms.reshape((-1,) + terms.shape[2:]) * factor
        part = lax.psum_scatter(terms, "seq", scatter_dimension=0, tiled=True)
        return lax.psum_scatter(part, "dp", scatter_dimension=0, tiled=True)

    return input_grad, scattered(conv), scattered(out), scattered(bias)


def solution(mesh):
    return jax.shard_map(
        functools.partial(local, mesh.shape["seq"], mesh.shape["dp"]),
        mesh=mesh,
        in_specs=(P("dp", "seq", None),) * 3 + (P(), P(), P()),
        out_specs=(P("dp", "seq", None), P(("seq", "dp"), None), P(("seq", "dp"), None), P(("seq", "dp"))),
        check_vma=False,
    )
```

```python
import functools
import math

import jax
import jax.numpy as jnp
from jax import lax
from jax.experimental import pallas as pl
from jax.experimental.pallas import tpu as pltpu
from jax.sharding import PartitionSpec as P

F32, BF16 = jnp.float32, jnp.bfloat16
NN = (((1,), (0,)), ((), ()))
TILE = 256


def unrolled(start, stop):
    return lambda body: [body(n) for n in range(start, stop)]


def aligned(value, size):
    return value if isinstance(value, int) else pl.multiple_of(value, size)


def split(value):
    high = value.astype(BF16)
    return high, (value - high.astype(F32)).astype(BF16)


def dot3(left, right, dims):
    product = functools.partial(lax.dot_general, dimension_numbers=dims, preferred_element_type=F32)
    (lh, ll), (rh, rl) = left, right
    return (product(ll, rh) + product(lh, rl)) + product(lh, rh)


def kernel(n_seq, n_dp, fused, factor, *refs):
    refs = list(refs)
    x, c2_in, sk_in, cw_in, cb, ow_in = refs[:6]
    ig, conv_o, out_o, bias_o = refs[6:10]
    (wch, wcl, woh, wol, wcth, wctl, woth, wotl, jh, jl, jth, jtl, hh, hl, fa, ga, oth, otl, dhs, dzh, dzl,
     x2, x2p, tail, q2, q2r, q1, q1r, c1, bsum, c2, sk, cw, ow, ssem, rsem, lsem) = refs[10:47]
    if fused:
        grad, rc, r1, r2, rz, rf = refs[47:53]
        bias_refs, sums = refs[53:59], refs[59]
    rows, chan = x.shape[1], x.shape[2]
    half = rows // 2
    gate = ow_in.shape[1]
    A, B = pl.ds(0, half), pl.ds(half, half)

    seq, dp = lax.axis_index("seq"), lax.axis_index("dp")
    has_next, has_prev = seq < n_seq - 1, seq > 0
    nxt, prv = lax.rem(seq + 1, n_seq), lax.rem(seq + n_seq - 1, n_seq)
    me_z, me_y, me_x, me_c = seq // 2, seq % 2, dp // 2, dp % 2

    fetches = {}
    for i, (name, src, dst) in enumerate((
        ("cw0", cw_in.at[0], cw.at[0]), ("ow0", ow_in.at[0], ow.at[0]), ("sk", sk_in, sk),
        ("c2", c2_in, c2), ("ow1", ow_in.at[1], ow.at[1]), ("cw1", cw_in.at[1], cw.at[1]))):
        fetches[name] = pltpu.make_async_copy(src, dst, lsem.at[i])
        fetches[name].start()

    barrier = pltpu.get_barrier_semaphore()
    greet = [(nxt, dp), (prv, dp)]
    if fused:
        greet += [(seq, 2 * me_x + 1 - me_c), (seq, 2 * (1 - me_x) + me_c), (2 * me_z + 1 - me_y, dp)]
        greet += [(lax.rem(seq + 2 * k, n_seq), dp) for k in range(1, n_seq // 2)]
    for s, d in greet:
        pl.semaphore_signal(barrier, inc=1, device_id=(s, d), device_id_type=pl.DeviceIdType.MESH)
    pl.semaphore_wait(barrier, len(greet))

    def remote(src, dst, send, recv, s, d):
        return pltpu.make_async_remote_copy(
            src_ref=src, dst_ref=dst, send_sem=ssem.at[send], recv_sem=rsem.at[recv],
            device_id=(s, d), device_id_type=pl.DeviceIdType.MESH)

    t_copy = remote(x.at[0, B], tail, 0, 0, nxt, dp)
    x2_copy = [remote(x2.at[r], x2p.at[r], 1 + i, 1 + i, nxt, dp) for i, r in enumerate((A, B))]
    q2_copy = [remote(q2.at[r], q2r.at[r], 3 + i, 3 + i, prv, dp) for i, r in enumerate((A, B))]
    q1_copy = remote(q1.at[A], q1r, 5, 5, prv, dp)

    pl.when(has_next)(t_copy.start)

    @pl.when(jnp.logical_not(has_prev))
    def _():
        tail[...] = jnp.zeros_like(tail)
        x2p[...] = jnp.zeros_like(x2p)

    @pl.when(jnp.logical_not(has_next))
    def _():
        q2r[...] = jnp.zeros_like(q2r)
        q1r[...] = jnp.zeros_like(q1r)

    def tiled(extent, body, size=TILE):
        @pl.loop(0, extent // size)
        def _(n):
            body(pl.ds(aligned(n * size, size), size))

    def split_conv(l):
        fetches["cw%d" % l].wait()

        def body(r):
            wch[l, r, :], wcl[l, r, :] = split(cw[l, r, :])
        tiled(2 * chan, body, 64)

    def split_out(l):
        fetches["ow%d" % l].wait()

        def body(r):
            woh[l, r, :], wol[l, r, :] = split(ow[l, r, :])
        tiled(gate, body, 64)

    def turn_conv(l):
        def body(r):
            wcth[l, r, :], wctl[l, r, :] = split(cw[l, :, r].T)
        tiled(2 * gate, body)

    def turn_out(l):
        def body(r):
            woth[l, r, :], wotl[l, r, :] = split(ow[l, :, r].T)
        tiled(2 * chan, body)

    def put_rows(l, r, c0, value):
        cols = pl.ds(c0, chan)
        jh[l, r, cols], jl[l, r, cols] = split(value)

    def put_turned(l, r, c0, value):
        cols = pl.ds(c0, chan)
        jth[l, cols, r], jtl[l, cols, r] = split(value.T)

    def put_outer(l, r, c0, value):
        cols = pl.ds(c0, chan)
        oth[l, cols, r], otl[l, cols, r] = split(value.T)

    def forward(l, r):
        @unrolled(0, gate // TILE)
        def _(n):
            joined = (jh[l, r, :], jl[l, r, :])
            cols = pl.ds(aligned(n * TILE, TILE), TILE)
            gcols = pl.ds(aligned(gate + n * TILE, TILE), TILE)
            f = dot3(joined, (wch[l, :, cols], wcl[l, :, cols]), NN) + cb[l:l + 1, cols]
            g = dot3(joined, (wch[l, :, gcols], wcl[l, :, gcols]), NN) + cb[l:l + 1, gcols]
            t, s = jnp.tanh(f), jax.nn.sigmoid(g)
            h = t * s
            fa[l, r, cols] = s * (1.0 - t * t)
            ga[l, r, cols] = h * (1.0 - s)
            hh[l, r, cols], hl[l, r, cols] = split(h)

    def second_input(r):
        out = pl.ds(0, chan)
        value = x[0, r, :] + dot3((hh[0, r, :], hl[0, r, :]), (woh[0, :, out], wol[0, :, out]), NN)
        x2[r, :] = value
        return value

    def dmixed(l, r):
        @unrolled(0, gate // TILE)
        def _(n):
            cols = pl.ds(aligned(n * TILE, TILE), TILE)
            gcols = pl.ds(aligned(gate + n * TILE, TILE), TILE)
            dh = dhs[l, r, cols]
            for part, where in ((dh * fa[l, r, cols], cols), (dh * ga[l, r, cols], gcols)):
                dzh[l, r, where], dzl[l, r, where] = split(part)
                total = jnp.sum(part, axis=0, keepdims=True)
                bsum[l, 0:1, where] = bsum[l, 0:1, where] + total

    def back(l, r, c0):
        taps = pl.ds(c0, chan)
        return dot3((dzh[l, r, :], dzl[l, r, :]), (wcth[l, :, taps], wctl[l, :, taps]), NN)

    n_out, n_conv = gate // TILE, 2 * gate // TILE
    tiles = n_out + n_conv

    def put_grad(l, kind, n, value):
        if not fused:
            (conv_o if kind == 0 else out_o)[l, :, pl.ds(aligned(n * TILE, TILE), TILE)] = value
            return
        block = value.shape[0] // 16
        for j in range(16):
            grad[l, kind * n_conv + n, j % 2, j // 2 % 2, j // 4 % 2, j // 8] = value[j * block:(j + 1) * block]

    def gradients(l):
        @pl.loop(0, n_out)
        def _(n):
            cols = pl.ds(aligned(n * TILE, TILE), TILE)
            put_grad(l, 1, n, dot3((oth[l], otl[l]), (hh[l, :, cols], hl[l, :, cols]), NN))
            step(l, n_conv + n, 0, "core")

        @pl.loop(0, n_conv)
        def _(n):
            cols = pl.ds(aligned(n * TILE, TILE), TILE)
            put_grad(l, 0, n, dot3((jth[l], jtl[l]), (dzh[l, :, cols], dzl[l, :, cols]), NN))
            step(l, n, 0, "core")

        total = bsum[l, 0:1, :]
        if not fused:
            bias_o[l:l + 1, :] = total
            return
        piece, terms = 2 * gate // 16, bias_refs[0]
        terms[l] = jnp.zeros(terms.shape[1:], F32)
        for j in range(16):
            terms[l, j % 2, j // 2 % 2, j // 4 % 2, j // 8, 0:1, 0:piece] = total[:, j * piece:(j + 1) * piece]
        step(l, None, 0, "core")

    def step(l, k, odd, what):
        if not fused:
            return
        if k is None:
            mine, got_c, got_1, got_2, got_z, got_f = (ref.at[l] for ref in bias_refs)
            base = 6 + 6 * (2 * tiles + l)
        else:
            mine, got_c, got_1, got_2, got_z, got_f = (ref.at[l, k] for ref in (grad, rc, r1, r2, rz, rf))
            base = 6 + 6 * (tiles * l + k)
        other_c = (seq, 2 * me_x + 1 - me_c)
        other_x = (seq, 2 * (1 - me_x) + me_c)
        other_y = (2 * me_z + 1 - me_y, dp)
        place = me_z if l == 0 else 3 - me_z
        low = lambda p: p if l == 0 else 1 - p
        at_place = lambda p: (2 * (p if l == 0 else 3 - p) + me_y, dp)
        own = mine.at[me_c]
        last = own.at[me_x, me_y]
        core = remote(mine.at[1 - me_c], got_c, base, base, *other_c)
        if odd:
            first = remote(own.at[:, 1 - me_y], got_1, base + 1, base + 1, *other_y)
            second = remote(own.at[1 - me_x, me_y], got_2, base + 2, base + 2, *other_x)
        else:
            first = remote(own.at[1 - me_x], got_1, base + 1, base + 1, *other_x)
            second = remote(own.at[me_x, 1 - me_y], got_2, base + 2, base + 2, *other_y)
        to_1, to_2 = (remote(last, got_z, base + 3, base + 3, *at_place(p)) for p in (1, 2))
        up = remote(last.at[low(0)], got_f, base + 3, base + 4, *at_place(0))
        down = remote(last.at[low(1)], got_f, base + 3, base + 4, *at_place(1))

        def finish(p):
            total = (last[low(p)] + got_f[...]) * factor
            if k is None:
                bias_o[...] = total
            else:
                sums[k] = total

        if what == "core":
            core.start()
        elif what == "first":
            core.wait_recv()
            own[...] += got_c[...]
            first.start()
        elif what == "second":
            first.wait_recv()
            if odd:
                own[:, me_y] += got_1[...]
            else:
                own[me_x] += got_1[...]
            second.start()
        elif what == "z":
            second.wait_recv()
            last[...] += got_2[...]
            pl.when(place == 3)(to_2.start)
            pl.when(place == 0)(down.start)
        elif what == "relay":
            @pl.when(place == 2)
            def _():
                to_2.wait_recv()
                last[...] += got_z[...]
                to_1.start()
        elif what == "owner":
            @pl.when(place == 1)
            def _():
                to_1.wait_recv()
                last[...] += got_z[...]
                up.start()
                down.wait_recv()
                finish(1)
        elif what == "end":
            @pl.when(place == 0)
            def _():
                up.wait_recv()
                finish(0)
                down.wait_send()

            pl.when(place == 1)(up.wait_send)
            pl.when(place == 2)(to_1.wait_send)
            pl.when(place == 3)(to_2.wait_send)
            core.wait_send()
            first.wait_send()
            second.wait_send()

    def advance(*moves):
        if not fused:
            return
        longest = max(behind for _, _, behind in moves)

        @pl.loop(0, tiles // 2 + longest)
        def _(tick):
            for l, what, behind in moves:
                def body(l=l, what=what, behind=behind):
                    for odd in range(2):
                        step(l, 2 * (tick - behind) + odd, odd, what)
                if longest == 0:
                    body()
                else:
                    pl.when(jnp.logical_and(tick >= behind, tick < behind + tiles // 2))(body)

        for l, what, _ in moves:
            step(l, None, 0, what)

    bsum[...] = jnp.zeros_like(bsum)
    every = pl.ds(0, rows)
    put_rows(0, B, 0, x[0, A, :])
    put_rows(0, B, chan, x[0, B, :])
    split_conv(0)
    forward(0, B)
    split_out(0)
    second_b = second_input(B)
    pl.when(has_next)(x2_copy[1].start)
    put_rows(0, A, chan, x[0, A, :])
    put_rows(1, B, chan, second_b)
    late, early = pl.ds(chan, chan), pl.ds(0, chan)
    turn_out(0)
    fetches["sk"].wait()
    skip = split(sk[0])
    dhs[0] = dot3(skip, (woth[0, late, :], wotl[0, late, :]), NN)
    pl.when(has_prev)(t_copy.wait_recv)
    put_rows(0, A, 0, tail[...])
    forward(0, A)
    second_a = second_input(A)
    pl.when(has_next)(x2_copy[0].start)
    put_rows(1, A, chan, second_a)
    split_conv(1)
    split_out(1)
    turn_out(1)
    fetches["c2"].wait()
    dhs[1] = dot3(skip, (woth[1, late, :], wotl[1, late, :]), NN) + dot3(
        split(c2[0]), (woth[1, early, :], wotl[1, early, :]), NN)
    turn_conv(1)
    def half_copy(src, dst, base, i, peer):
        r = pl.ds(aligned(i * half, half), half)
        return r, remote(src.at[r], dst.at[r], base + i, base + i, peer, dp)

    @unrolled(0, 2)
    def _(n):
        r, landed = half_copy(x2, x2p, 1, 1 - n, nxt)
        pl.when(has_prev)(landed.wait_recv)
        put_rows(1, r, 0, x2p[r, :])
        forward(1, r)
        dmixed(1, r)
        q2[r, :] = back(1, r, 0)
        _, leaving = half_copy(q2, q2r, 3, 1 - n, prv)
        pl.when(has_prev)(leaving.start)

    @unrolled(0, 2)
    def _(n):
        r = pl.ds(aligned(n * half, half), half)
        for l in range(2):
            put_outer(l, r, chan, sk[0, r, :])
        put_outer(1, r, 0, c2[0, r, :])
        put_turned(1, r, 0, x2p[r, :])
        put_turned(1, r, chan, x2[r, :])

    gradients(1)

    @unrolled(0, 2)
    def _(n):
        r = pl.ds(aligned(n * half, half), half)
        c1[r, :] = c2[0, r, :] + back(1, r, chan)
        put_turned(0, r, chan, x[0, r, :])

    turn_conv(0)
    put_turned(0, B, 0, x[0, A, :])
    put_turned(0, A, 0, tail[...])
    advance((1, "first", 0))

    @unrolled(0, 2)
    def _(n):
        r, landed = half_copy(q2, q2r, 3, 1 - n, prv)
        pl.when(has_next)(landed.wait_recv)
        carried = c1[r, :] + q2r[r, :]
        c1[r, :] = carried
        dhs[0, r, :] += dot3(split(carried), (woth[0, early, :], wotl[0, early, :]), NN)
        dmixed(0, r)
        q1[r, :] = back(0, r, 0)

    pl.when(has_prev)(q1_copy.start)

    @unrolled(0, 2)
    def _(n):
        r = pl.ds(aligned(n * half, half), half)
        put_outer(0, r, 0, c1[r, :])

    gradients(0)
    advance((0, "first", 0))
    advance((1, "second", 0))

    @unrolled(0, 2)
    def _(n):
        r = pl.ds(aligned(n * half, half), half)
        c1[r, :] += back(0, r, chan)

    ig[0, A, :] = c1[A, :] + q1[B, :]
    pl.when(has_next)(q1_copy.wait_recv)
    ig[0, B, :] = c1[B, :] + q1r[...]
    advance((1, "z", 0), (0, "second", 0), (1, "relay", 1), (0, "z", 1), (1, "owner", 2), (0, "relay", 2))
    advance((0, "owner", 0))
    advance((0, "end", 0))
    advance((1, "end", 0))
    if fused:
        for n in range(n_conv):
            conv_o[:, n * TILE:(n + 1) * TILE] = sums[n]
        for n in range(n_out):
            out_o[:, n * TILE:(n + 1) * TILE] = sums[n_conv + n]
    pl.when(has_next)(t_copy.wait_send)
    for i in range(2):
        pl.when(has_next)(x2_copy[i].wait_send)
        pl.when(has_prev)(q2_copy[i].wait_send)
    pl.when(has_prev)(q1_copy.wait_send)


def hand_on(a, b, c, bias, a_out, b_out, c_out, bias_out):
    a_out[...], b_out[...], c_out[...] = a[...], b[...], c[...]
    bias_out[...] = bias[0, : bias_out.shape[0]]


def local(n_seq, n_dp, *args):
    inputs, _, _, convolution_weight, _, output_weight = args
    _, rows, chan = inputs.shape
    half = rows // 2
    gate = output_weight.shape[1]
    fused = (n_seq, n_dp) == (8, 4)
    factor = 1.0 / math.sqrt(rows * n_seq * n_dp)
    block = 2 * (2 * chan) // (n_seq * n_dp)
    vmem, sds = pltpu.VMEM, jax.ShapeDtypeStruct
    if fused:
        grads = [sds((block, 2 * gate), F32), sds((block, gate), F32), sds((8, 128), F32)]
    else:
        grads = [sds((2, 2 * chan, 2 * gate), F32), sds((2, 2 * chan, gate), F32), sds((2, 2 * gate), F32)]
    pair = lambda *shape: [vmem(shape, BF16)] * 2
    scratch = [
        *pair(2, 2 * chan, 2 * gate), *pair(2, gate, 2 * chan),
        *pair(2, 2 * gate, 2 * chan), *pair(2, 2 * chan, gate),
        *pair(2, rows, 2 * chan), *pair(2, 2 * chan, rows), *pair(2, rows, gate),
        vmem((2, rows, gate), F32), vmem((2, rows, gate), F32),
        *pair(2, 2 * chan, rows), vmem((2, rows, gate), F32), *pair(2, rows, 2 * gate),
        vmem((rows, chan), F32), vmem((rows, chan), F32), vmem((half, chan), F32),
        vmem((rows, chan), F32), vmem((rows, chan), F32), vmem((rows, chan), F32),
        vmem((half, chan), F32), vmem((rows, chan), F32), vmem((2, 8, 2 * gate), F32),
        vmem(inputs.shape, F32), vmem(inputs.shape, F32),
        vmem(convolution_weight.shape, F32), vmem(output_weight.shape, F32),
        pltpu.SemaphoreType.DMA((18 + 36 * gate // TILE,)), pltpu.SemaphoreType.DMA((18 + 36 * gate // TILE,)),
        pltpu.SemaphoreType.DMA((6,)),
    ]
    if fused:
        tiles = 3 * gate // 256
        for lead, tile in (((2, tiles), (block, 256)), ((2,), (8, 128))):
            for between in ((2, 2, 2, 2), (2, 2, 2), (2, 2), (2,), (2,), ()):
                scratch.append(vmem(lead + between + tile, F32))
        scratch.append(vmem((tiles, block, 256), F32))
    spec, anywhere = pl.BlockSpec(memory_space=pltpu.VMEM), pl.BlockSpec(memory_space=pl.ANY)
    input_grad, conv, out, bias = pl.pallas_call(
        functools.partial(kernel, n_seq, n_dp, fused, factor),
        out_shape=[sds(inputs.shape, F32)] + grads,
        in_specs=[spec, anywhere, anywhere, anywhere, spec, anywhere],
        out_specs=[spec] * 4,
        scratch_shapes=scratch,
        compiler_params=pltpu.CompilerParams(
            collective_id=0, has_side_effects=True, vmem_limit_bytes=60 * 1024 * 1024),
    )(*args)
    if fused:
        piece = 4 * gate // (n_seq * n_dp)
        return pl.pallas_call(
            hand_on,
            out_shape=[sds(inputs.shape, F32), *grads[:2], sds((piece,), F32)],
            in_specs=[spec] * 4,
            out_specs=[spec] * 4,
        )(input_grad, conv, out, bias)

    def scattered(terms):
        terms = terms.reshape((-1,) + terms.shape[2:]) * factor
        part = lax.psum_scatter(terms, "seq", scatter_dimension=0, tiled=True)
        return lax.psum_scatter(part, "dp", scatter_dimension=0, tiled=True)

    return input_grad, scattered(conv), scattered(out), scattered(bias)


def solution(mesh):
    return jax.shard_map(
        functools.partial(local, mesh.shape["seq"], mesh.shape["dp"]),
        mesh=mesh,
        in_specs=(P("dp", "seq", None),) * 3 + (P(), P(), P()),
        out_specs=(P("dp", "seq", None), P(("seq", "dp"), None), P(("seq", "dp"), None), P(("seq", "dp"))),
        check_vma=False,
    )
```
